256 devices in a mesh: lat: 16 (over z, y_hi), lon: 16 (over x, y_lo, core).
Axes of the slice: x: 4, y: 4 (y_hi: 2, y_lo: 2; y = y_hi * 2 + y_lo), z: 8, core: 2. Of those that a mesh axis runs over, the one named last changes fastest.
Arguments:
- fields: bfloat16 [128, 1440, 256], P('lat', 'lon'), may hold values from -6 to 6
- lat_mask: int32 [128], P('lat'), may hold values from 0 to 1, as said below
- conv_first: bfloat16 [2, 3, 3, 256, 256], replicated, may hold values from -0.125 to 0.125
- conv_second: bfloat16 [2, 3, 3, 256, 256], replicated, may hold values from -0.125 to 0.125
- norm_gain: float32 [2, 256], replicated, may hold values from 0.1 to 1.9
- qkv_weight: bfloat16 [2, 256, 768], replicated, may hold values from -0.375 to 0.375
- out_weight: bfloat16 [2, 256, 256], replicated, may hold values from -1.5 to 1.5
Outputs:
- result: bfloat16 [128, 1440, 256], P('lat', 'lon')
The draws below stay inside these ranges and needn't reach their ends.
Inputs may be any that keep to these rules, and one draw needn't show every extreme that they name: lat_mask is 1 on the first latitude rows and 0 on the rest; between 1 and 12 rows are 0.
All inputs are finite; a program needn't handle non-finite values.
Results may differ from the reference program's by a relative error of at most 0.013.
Values may be sent and summed in bfloat16 or wider, within the bound.
A program may use at most 128 MiB of HBM per device.

```python
import jax
import jax.numpy as jnp
from jax import lax

C = 256
HEADS = 4
BLOCKS = 2
LAT_DEV = 8
LAT = 128
LON = 1440


def draw_lat_mask(key, part):
    padding = jax.random.randint(key, (), 1, LAT_DEV + LAT_DEV // 2 + 1)
    positions = jnp.arange(LAT)
    return (positions < LAT - padding).astype(jnp.int32)


def levels(rng, shape, pieces, smallest, high):
    loudness = 1.0
    for position, shards_of in pieces:
        steps = jax.random.uniform(jax.random.fold_in(jax.random.fold_in(rng, 6), position), (shards_of,), jnp.float32, smallest / len(pieces), high / len(pieces))
        loudness = loudness * jnp.repeat(jnp.exp(steps), shape[position] // shards_of).reshape((-1,) + (1,) * (len(shape) - 1 - position))
    return loudness


def centred(key, extent, scale, most, cuts=(), dtype=jnp.bfloat16):
    level = levels(key, extent, cuts, -0.22, 0.18) if cuts else 1.0
    drawn = jax.random.normal(key, extent, jnp.float32) * scale * level
    return jnp.minimum(jnp.maximum(drawn, -most), most).astype(dtype)


def setup_inputs(seed: int = 0) -> dict:
    key_list = jax.random.split(jax.random.key(seed), 8)
    return {
        "fields": centred(key_list[0], (LAT, LON, C), 1.0, 6.0, ((0, 16), (1, 16))),
        "lat_mask": draw_lat_mask(jax.random.fold_in(key_list[7], 71), 0),
        "conv_first": centred(key_list[2], (BLOCKS, 3, 3, C, C), (9 * C) ** -0.5, 0.125),
        "conv_second": centred(key_list[3], (BLOCKS, 3, 3, C, C), (9 * C) ** -0.5, 0.125),
        "norm_gain": jnp.clip(1.0 + 0.18 * jax.random.normal(key_list[4], (BLOCKS, C), jnp.float32), 0.1, 1.9),
        "qkv_weight": centred(key_list[5], (BLOCKS, C, 3 * C), C ** -0.5, 0.375),
        "out_weight": centred(key_list[6], (BLOCKS, C, C), (C // 16) ** -0.5, 1.5),
    }


def convolve(values, kernel, spread):
    rows, cols = (values.shape[0], values.shape[1])
    padded = jnp.pad(values, ((spread, spread), (0, 0), (0, 0)))
    padded = jnp.pad(padded, ((0, 0), (spread, spread), (0, 0)), mode='wrap')
    total = jnp.zeros((rows, cols, values.shape[2]), jnp.float32)
    for i in range(3):
        for j in range(3):
            window = padded[i * spread:i * spread + rows, j * spread:j * spread + cols]
            total = total + jnp.dot(window, kernel[i, j], preferred_element_type=jnp.float32)
    return total

def row_attention(qkv_row):
    width = qkv_row.shape[1] // 3
    head_dim = width // HEADS
    query = qkv_row[:, :width].reshape(-1, HEADS, head_dim).astype(jnp.float32)
    keys = qkv_row[:, width:2 * width].reshape(-1, HEADS, head_dim).astype(jnp.float32)
    vals = qkv_row[:, 2 * width:].reshape(-1, HEADS, head_dim).astype(jnp.float32)
    scores = jnp.einsum('qhd,khd->hqk', query, keys) / jnp.sqrt(jnp.float32(head_dim))
    expo = jnp.exp(scores)
    total = lax.optimization_barrier(jnp.sum(expo, axis=-1))
    weights = expo.astype(jnp.bfloat16).astype(jnp.float32)
    summed = jnp.einsum('hqk,khd->hqd', weights, vals) / total[..., None]
    return jnp.transpose(summed, (1, 0, 2)).reshape(-1, width).astype(jnp.bfloat16)

def reference(fields, lat_mask, conv_first, conv_second, norm_gain, qkv_weight, out_weight):
    mask_f = lat_mask.astype(jnp.float32)[:, None, None]
    state = (fields.astype(jnp.float32) * mask_f).astype(jnp.bfloat16)
    for blk in range(BLOCKS):
        hidden = (jax.nn.gelu(convolve(state, conv_first[blk], 1)) * mask_f).astype(jnp.bfloat16)
        mid = ((state.astype(jnp.float32) + jax.nn.gelu(convolve(hidden, conv_second[blk], 2))) * mask_f).astype(jnp.bfloat16)
        midf = mid.astype(jnp.float32)
        mean = lax.optimization_barrier(jnp.mean(midf, axis=-1, keepdims=True))
        var = lax.optimization_barrier(jnp.mean((midf - mean) ** 2, axis=-1, keepdims=True))
        normed = ((midf - mean) / jnp.sqrt(var + 1e-05) * norm_gain[blk]).astype(jnp.bfloat16)
        qkv = jnp.dot(normed, qkv_weight[blk], preferred_element_type=jnp.float32).astype(jnp.bfloat16)
        attended = lax.map(row_attention, qkv)
        update = jnp.dot(attended, out_weight[blk], preferred_element_type=jnp.float32)
        state = ((midf + update) * mask_f).astype(jnp.bfloat16)
    return state
```

```python
import math

import jax
import jax.numpy as jnp
from jax import lax
from jax.experimental import pallas as pl
from jax.experimental.pallas import tpu as pltpu
from jax.sharding import PartitionSpec as P

HEADS = 4
BLOCKS = 2
EDGE = 3
CORES = 2
BF = jnp.bfloat16
F32 = jnp.float32
MESH = pl.DeviceIdType.MESH


def conv(src, start, count, spread, weights):
    wide, width = src.shape[1], src.shape[2]
    cells = count * wide
    taps = [src[pl.ds(start + i * spread, count)].reshape(cells, width) for i in range(3)]
    lhs = jnp.concatenate(taps, axis=1)
    parts = [
        jnp.dot(lhs, weights[:, j].reshape(3 * width, width), preferred_element_type=F32)
        for j in range(3)
    ]
    return pltpu.roll(parts[0], spread, 0) + parts[1] + pltpu.roll(parts[2], cells - spread, 0)


def kernel(
    fields, mask, w1_hbm, w2_hbm, gain, wqkv_hbm, wo_hbm, out,
    w1, w2, wqkv, wo, xs, xb, hb, mb, midb, epack, erecv, nself, nbuf, qb, kb, vx, att, abuf,
    wsem, e_send, e_recv, l_send, l_recv, m_sem, f_send, f_recv, s_send, s_recv, r_send, r_recv,
):
    rows, cols, width = fields.shape
    wide = cols + 2 * EDGE
    head_dim = width // HEADS
    lats, lons = lax.axis_size("lat"), lax.axis_size("lon")
    chips = lons // CORES
    groups = chips // 2
    half = chips * wide
    lat, lon = lax.axis_index("lat"), lax.axis_index("lon")
    chip, core = lon // CORES, lon % CORES
    group = chip // 2
    up, down = (lat + lats - 1) % lats, (lat + 1) % lats
    left, right = (lon + lons - 1) % lons, (lon + 1) % lons
    sibling = chip * CORES + 1 - core
    beyond = (lon + lons - 1 + 2 * core) % lons

    def remote(src, dst, send, recv, to):
        return pltpu.make_async_remote_copy(
            src_ref=src, dst_ref=dst, send_sem=send, recv_sem=recv, device_id=to, device_id_type=MESH
        )

    def each(count, body):
        lax.fori_loop(0, count, lambda k, carry: (body(k), carry)[1], 0)

    barrier = pltpu.get_barrier_semaphore()

    def greet(to):
        pl.semaphore_signal(barrier, inc=1, device_id=to, device_id_type=MESH)

    greet((up, lon))
    greet((down, lon))
    greet((lat, sibling))
    greet((lat, beyond))
    each(chips - 1, lambda k: greet((lat, (chip + 1 + k) % chips * CORES + core)))

    def weight_copies(blk):
        return [
            pltpu.make_async_copy(w1_hbm.at[blk], w1.at[blk], wsem.at[0, blk]),
            pltpu.make_async_copy(w2_hbm.at[blk], w2.at[blk], wsem.at[1, blk]),
            pltpu.make_async_copy(wqkv_hbm.at[blk], wqkv.at[blk], wsem.at[2, blk]),
            pltpu.make_async_copy(wo_hbm.at[blk], wo.at[blk], wsem.at[3, blk]),
        ]

    for blk in range(BLOCKS):
        for copy in weight_copies(blk):
            copy.start()

    xs[...] = jnp.zeros_like(xs)
    for a in range(rows):
        on = mask[a].astype(F32)
        mb[EDGE + a] = jnp.full(mb.shape[1:], on, F32)
        xs[a, EDGE : EDGE + cols, :] = fields[a].astype(F32) * on
    xb[0, EDGE : EDGE + rows] = xs[...].astype(BF)
    mb[0:EDGE] = jnp.full((EDGE,) + mb.shape[1:], jnp.where(lat > 0, 1.0, 0.0), F32)

    pl.semaphore_wait(barrier, chips + 3)

    def mask_copy():
        return remote(
            mb.at[pl.ds(EDGE, EDGE)], mb.at[pl.ds(EDGE + rows, EDGE)], m_sem.at[0], m_sem.at[1], (up, lon)
        )

    mask_copy().start()

    def row_mask(first, count):
        on = mb[pl.ds(first, count)][:, :1, :]
        return jnp.concatenate([on, on], axis=2)

    column = lax.broadcasted_iota(jnp.int32, (1, wide, 1), 1)
    inside = (column >= EDGE) & (column < EDGE + cols)

    def block(blk):
        x = xb.at[blk]
        own = pl.ds(EDGE, rows)
        w1_copy, w2_copy, wqkv_copy, wo_copy = weight_copies(blk)

        low = x[own, 0:16, :].astype(F32)
        high = x[own, wide - 16 : wide, :].astype(F32)
        epack[blk, 0] = pltpu.roll(low[:, 0:8], 2, 1).reshape(rows * 8, width).astype(BF)
        epack[blk, 1] = pltpu.roll(high[:, 8:16], 6, 1).reshape(rows * 8, width).astype(BF)

        def edge_copies():
            return [
                remote(epack.at[blk, 0], erecv.at[blk, 1], e_send.at[blk, 0], e_recv.at[blk, 1], (lat, left)),
                remote(epack.at[blk, 1], erecv.at[blk, 0], e_send.at[blk, 1], e_recv.at[blk, 0], (lat, right)),
            ]

        for copy in edge_copies():
            copy.start()
        for copy in edge_copies():
            copy.wait_recv()
        place = lax.broadcasted_iota(jnp.int32, (rows, 16, width), 1)
        nothing = jnp.zeros((rows, 8, width), F32)
        from_left = erecv[blk, 0].astype(F32).reshape(rows, 8, width)
        from_right = erecv[blk, 1].astype(F32).reshape(rows, 8, width)
        x[own, 0:16, :] = jnp.where(
            place < EDGE, jnp.concatenate([from_left, nothing], axis=1), low
        ).astype(BF)
        x[own, wide - 16 : wide, :] = jnp.where(
            place >= 16 - EDGE, jnp.concatenate([nothing, from_right], axis=1), high
        ).astype(BF)

        def row_copies():
            top, bottom = pl.ds(EDGE, EDGE), pl.ds(rows, EDGE)
            above, below = pl.ds(0, EDGE), pl.ds(EDGE + rows, EDGE)
            return [
                remote(x.at[top], x.at[below], l_send.at[blk, 0], l_recv.at[blk, 1], (up, lon)),
                remote(x.at[bottom], x.at[above], l_send.at[blk, 1], l_recv.at[blk, 0], (down, lon)),
            ]

        for copy in row_copies():
            copy.start()

        w1_copy.wait()

        def first(start):
            got = conv(x, start, EDGE, 1, w1.at[blk])
            got = jax.nn.gelu(got).reshape(EDGE, wide, width) * row_mask(start + 1, EDGE)
            hb[pl.ds(start, EDGE)] = got.astype(BF)

        each(2, lambda k: first(EDGE * (1 + k)))
        for copy in row_copies():
            copy.wait_recv()

        @pl.when(blk == 0)
        def _():
            mask_copy().wait_recv()

        @pl.when(lat == 0)
        def _():
            x[0:EDGE] = jnp.zeros((EDGE, wide, width), BF)

        @pl.when(lat == lats - 1)
        def _():
            x[EDGE + rows :] = jnp.zeros((EDGE, wide, width), BF)
            mb[EDGE + rows :] = jnp.zeros((EDGE,) + mb.shape[1:], F32)

        each(2, lambda k: first(3 * EDGE * k))

        w2_copy.wait()

        def row_copy(r, to):
            return remote(
                nself.at[blk, r], nbuf.at[blk, core, chip], f_send.at[blk, r], f_recv.at[blk, chip],
                (lat, to * CORES + core),
            )

        def second(k):
            pair = (group + 1 + k) % groups
            a = pair * 2
            got = jax.nn.gelu(conv(hb, a, 2, 2, w2.at[blk])).reshape(2, wide, width)
            got = (x[pl.ds(a + EDGE, 2)].astype(F32) + got) * row_mask(a + EDGE, 2)
            got = got.astype(BF)
            midb[pl.ds(a, 2)] = got
            got = got.astype(F32)
            got = got - jnp.mean(got, axis=-1, keepdims=True)
            var = jnp.mean(got * got, axis=-1, keepdims=True)
            got = got * lax.rsqrt(var + 1e-05) * gain[blk]
            nself[blk, pl.ds(a, 2)] = jnp.where(inside, got, 0.0).astype(BF)
            for i in range(2):
                r = a + i

                @pl.when(r != chip)
                def _():
                    row_copy(r, r).start()

                @pl.when(r == chip)
                def _():
                    nbuf[blk, core, r] = nself[blk, r]

        each(groups, second)

        def half_copy(source):
            slot = nbuf.at[blk, core, source]
            return remote(slot, slot, s_send.at[blk, source], s_recv.at[blk, source], (lat, sibling))

        def pass_on(k):
            source = ((group + 2 * groups - 1 - k // 2) % groups) * 2 + k % 2

            @pl.when(source != chip)
            def _():
                remote(
                    nself.at[blk, source], nbuf.at[blk, core, source], f_send.at[blk, source],
                    f_recv.at[blk, source], (lat, source * CORES + core),
                ).wait_recv()

            half_copy(source).start()

        each(chips, pass_on)

        wqkv_copy.wait()
        mine = nbuf[blk, core].reshape(half, width)
        scale = math.log2(math.e) / math.sqrt(head_dim)
        query = jnp.dot(mine, wqkv[blk, :, 0:width], preferred_element_type=F32) * scale
        qb[...] = query.astype(BF).reshape(chips, wide, width)
        lane = lax.broadcasted_iota(jnp.int32, (1, 1, 2 * head_dim), 2)
        first_head = lane < head_dim
        ones = jnp.where(inside, 1.0, 0.0)

        def keys_values(t):
            side = (core + t) % CORES

            @pl.when(t == 1)
            def _():
                each(chips, lambda source: half_copy(source).wait_recv())

            cells = nbuf[blk, side].reshape(half, width)
            both = jnp.dot(cells, wqkv[blk, :, width:], preferred_element_type=F32)
            kb[side] = both[:, :width].astype(BF)
            values = both[:, width:].reshape(chips, wide, width)
            for h in range(HEADS):
                pair = values[:, :, h // 2 * 2 * head_dim :][:, :, : 2 * head_dim]
                keep = first_head if h % 2 == 0 else ~first_head
                vx[h, side] = jnp.where(keep, pair, ones).astype(BF).reshape(half, 2 * head_dim)

        each(CORES, keys_values)

        def back_copy(slot, row, to):
            return remote(
                att.at[blk, slot], abuf.at[blk, row], r_send.at[blk, slot], r_recv.at[blk, row],
                (lat, to * CORES + core),
            )

        def attend(k):
            pair = (group + 1 + k) % groups
            a = pair * 2
            query = qb[pl.ds(a, 2)].reshape(2 * wide, width)
            low_lane = lax.broadcasted_iota(jnp.int32, (1, 2 * head_dim), 1) < head_dim
            zero = jnp.zeros((), BF)
            for p in range(HEADS // 2):
                span = slice(p * 2 * head_dim, (p + 1) * 2 * head_dim)
                both = query[:, span]
                lhs = jnp.concatenate(
                    [jnp.where(low_lane, both, zero), jnp.where(low_lane, zero, both)], axis=0
                )
                keys = kb[:, :, span].reshape(CORES * half, 2 * head_dim)
                scores = lax.dot_general(
                    lhs, keys, (((1,), (1,)), ((), ())), preferred_element_type=F32
                )
                expo = jnp.exp2(scores).astype(BF)
                got = []
                for e in range(2):
                    values = vx[2 * p + e].reshape(CORES * half, 2 * head_dim)
                    part = jnp.dot(
                        expo[e * 2 * wide : (e + 1) * 2 * wide], values, preferred_element_type=F32
                    )
                    got.append(part / pltpu.roll(part, head_dim, 1))
                done = jnp.where(low_lane, got[0], got[1]).astype(BF)
                att[blk, pl.ds(a, 2), :, span] = done.reshape(2, wide, 2 * head_dim)
            for i in range(2):
                home = a + i

                @pl.when(home != chip)
                def _():
                    back_copy(home, chip, home).start()

                @pl.when(home == chip)
                def _():
                    abuf[blk, home] = att[blk, home]

        each(groups, attend)

        wo_copy.wait()

        def arrived(k):
            row = (chip + 1 + k) % chips
            back_copy(row, row, row).wait_recv()

        each(chips - 1, arrived)

        def project(k):
            a = k * 2
            cells = abuf[blk, pl.ds(a, 2)].reshape(2 * wide, width)
            got = jnp.dot(cells, wo[blk], preferred_element_type=F32).reshape(2, wide, width)
            got = (midb[pl.ds(a, 2)].astype(F32) + got) * row_mask(a + EDGE, 2)
            xb[blk + 1, pl.ds(a + EDGE, 2)] = got.astype(BF)

        each(rows // 2, project)

        for copy in edge_copies() + row_copies():
            copy.wait_send()

        def left_here(k):
            to = (chip + 1 + k) % chips
            row_copy(to, to).wait_send()
            back_copy(to, chip, to).wait_send()

        each(chips - 1, left_here)
        each(chips, lambda source: half_copy(source).wait_send())

    each(BLOCKS, block)
    mask_copy().wait_send()
    out[...] = xb[BLOCKS, EDGE : EDGE + rows]


def body(fields, lat_mask, conv_first, conv_second, norm_gain, qkv_weight, out_weight):
    rows, cols, width = fields.shape
    wide = cols + 2 * EDGE
    chips = lax.axis_size("lon") // CORES
    half = chips * wide
    head_dim = width // HEADS
    vmem = pl.BlockSpec(memory_space=pltpu.VMEM)
    hbm = pl.BlockSpec(memory_space=pl.ANY)
    dma = pltpu.SemaphoreType.DMA
    wide_out = pl.pallas_call(
        kernel,
        out_shape=jax.ShapeDtypeStruct((rows, wide, width), BF),
        in_specs=[vmem, pl.BlockSpec(memory_space=pltpu.SMEM), hbm, hbm, vmem, hbm, hbm],
        out_specs=vmem,
        scratch_shapes=[
            pltpu.VMEM(conv_first.shape, BF),
            pltpu.VMEM(conv_second.shape, BF),
            pltpu.VMEM(qkv_weight.shape, BF),
            pltpu.VMEM(out_weight.shape, BF),
            pltpu.VMEM((rows, wide, width), F32),
            pltpu.VMEM((BLOCKS + 1, rows + 2 * EDGE, wide, width), BF),
            pltpu.VMEM((rows + 4, wide, width), BF),
            pltpu.VMEM((rows + 2 * EDGE, 8, width // 2), F32),
            pltpu.VMEM((rows, wide, width), BF),
            pltpu.VMEM((BLOCKS, 2, rows * 8, width), BF),
            pltpu.VMEM((BLOCKS, 2, rows * 8, width), BF),
            pltpu.VMEM((BLOCKS, rows, wide, width), BF),
            pltpu.VMEM((BLOCKS, CORES, chips, wide, width), BF),
            pltpu.VMEM((chips, wide, width), BF),
            pltpu.VMEM((CORES, half, width), BF),
            pltpu.VMEM((HEADS, CORES, half, 2 * head_dim), BF),
            pltpu.VMEM((BLOCKS, chips, wide, width), BF),
            pltpu.VMEM((BLOCKS, rows, wide, width), BF),
            dma((4, BLOCKS)),
            dma((BLOCKS, 2)),
            dma((BLOCKS, 2)),
            dma((BLOCKS, 2)),
            dma((BLOCKS, 2)),
            dma((2,)),
            dma((BLOCKS, chips)),
            dma((BLOCKS, chips)),
            dma((BLOCKS, chips)),
            dma((BLOCKS, chips)),
            dma((BLOCKS, chips)),
            dma((BLOCKS, chips)),
        ],
        compiler_params=pltpu.CompilerParams(
            collective_id=0, has_side_effects=True, vmem_limit_bytes=50 * 1024 * 1024
        ),
    )(
        fields,
        lat_mask,
        conv_first,
        conv_second,
        norm_gain.reshape(BLOCKS, 1, width),
        qkv_weight,
        out_weight,
    )
    return wide_out[:, EDGE : EDGE + cols]


def solution(mesh):
    placed = (P("lat", "lon", None), P("lat"), P(), P(), P(), P(), P())
    return jax.shard_map(
        body, mesh=mesh, in_specs=placed, out_specs=P("lat", "lon", None), check_vma=False
    )
```

```python
import math

import jax
import jax.numpy as jnp
from jax import lax
from jax.experimental import pallas as pl
from jax.experimental.pallas import tpu as pltpu
from jax.sharding import PartitionSpec as P

HEADS = 4
BLOCKS = 2
EDGE = 3
CORES = 2
RING = 4
BF = jnp.bfloat16
F32 = jnp.float32
MESH = pl.DeviceIdType.MESH


def conv(src, start, count, spread, weights):
    wide, width = src.shape[1], src.shape[2]
    cells = count * wide
    taps = [src[pl.ds(start + i * spread, count)].reshape(cells, width) for i in range(3)]
    lhs = jnp.concatenate(taps, axis=1)
    parts = [
        jnp.dot(lhs, weights[:, j].reshape(3 * width, width), preferred_element_type=F32)
        for j in range(3)
    ]
    return pltpu.roll(parts[0], spread, 0) + parts[1] + pltpu.roll(parts[2], cells - spread, 0)


def shifted(cells, start, by):
    tile = cells[:, start // 16 * 16 : start // 16 * 16 + 16, :].astype(F32)
    return pltpu.roll(tile[:, start % 16 : start % 16 + 8], by, 1)


def with_edges(ref, index, from_left, from_right):
    count, _, width = from_left.shape
    wide = ref.shape[-2]
    place = lax.broadcasted_iota(jnp.int32, (count, 16, width), 1)
    nothing = jnp.zeros(from_left.shape, F32)
    low = ref[index, 0:16, :].astype(F32)
    high = ref[index, wide - 16 : wide, :].astype(F32)
    ref[index, 0:16, :] = jnp.where(
        place < EDGE, jnp.concatenate([from_left, nothing], axis=1), low
    ).astype(BF)
    ref[index, wide - 16 : wide, :] = jnp.where(
        place >= 16 - EDGE, jnp.concatenate([nothing, from_right], axis=1), high
    ).astype(BF)


def kernel(
    fields, mask, w1_hbm, w2_hbm, gain, wqkv_hbm, wo_hbm, out,
    w1, w2, wqkv, wo, xs, xb, hb, mp, epack, erecv, nself, nbuf, qm, kb, vx, att,
    wsem, e_send, e_recv, l_send, l_recv, m_sem, f_send, f_recv, s_send, s_recv, h_send, n_send, x_recv,
):
    rows, cols, width = fields.shape
    wide = cols + 2 * EDGE
    head_dim = width // HEADS
    lats, lons = lax.axis_size("lat"), lax.axis_size("lon")
    chips = lons // CORES
    groups = chips // 2
    half = chips * wide
    lat, lon = lax.axis_index("lat"), lax.axis_index("lon")
    chip, core = lon // CORES, lon % CORES
    z, y_hi = lat // 2, lat % 2
    x_at, y_at = lon // 4, y_hi * 2 + (lon // 2) % 2
    up, down = (lat + lats - 1) % lats, (lat + 1) % lats
    left, right = (lon + lons - 1) % lons, (lon + 1) % lons
    sibling = chip * CORES + 1 - core
    band_1, sector_1 = z * 2 + core, x_at * 4 + (y_at + x_at) % RING

    def place_1(band, sector):
        x = sector // 4
        y = (sector + 3 * x) % RING
        return band // 2 * 2 + y // 2, x * 4 + y % 2 * 2 + band % 2

    def placed(blk, band, sector):
        there = place_1(band, sector)
        return band + blk * (there[0] - band), sector + blk * (there[1] - sector)

    def elsewhere(to):
        return (to[0] != lat) | (to[1] != lon)

    def remote(src, dst, send, recv, to):
        return pltpu.make_async_remote_copy(
            src_ref=src, dst_ref=dst, send_sem=send, recv_sem=recv, device_id=to, device_id_type=MESH
        )

    def each(count, body):
        lax.fori_loop(0, count, lambda k, carry: (body(k), carry)[1], 0)

    def across(k):
        return (x_at + 2 - k + k // 2 * (2 * k - 1) + RING) % RING

    barrier = pltpu.get_barrier_semaphore()

    def greet(to):
        @pl.when(elsewhere(to))
        def _():
            pl.semaphore_signal(barrier, inc=1, device_id=to, device_id_type=MESH)

    def count(to):
        return jnp.where(elsewhere(to), 1, 0)

    def row_at(place):
        row = place - EDGE + rows
        return (band_1 + row // rows - 1 + lats) % lats, row % rows * CORES + sector_1 % 2

    beside = (lat + lats + chip // 5 - (7 - chip) // 5) % lats
    is_halo = (chip < EDGE) | (chip >= rows - EDGE)

    for to in ((up, lon), (down, lon), (lat, left), (lat, right), (lat, sibling)):
        greet(to)
    each(chips, lambda i: greet((lat, i * CORES + core)))
    each(chips, lambda i: greet(place_1(lat, i * CORES + core)))
    each(rows + 2 * EDGE, lambda place: greet(row_at(place)))

    def weight_copies(blk):
        return [
            pltpu.make_async_copy(w1_hbm.at[blk], w1.at[blk], wsem.at[0, blk]),
            pltpu.make_async_copy(w2_hbm.at[blk], w2.at[blk], wsem.at[1, blk]),
            pltpu.make_async_copy(wqkv_hbm.at[blk], wqkv.at[blk], wsem.at[2, blk]),
            pltpu.make_async_copy(wo_hbm.at[blk], wo.at[blk], wsem.at[3, blk]),
        ]

    for blk in range(BLOCKS):
        for copy in weight_copies(blk):
            copy.start()

    xs[...] = jnp.zeros_like(xs)
    for a in range(rows):
        on = mask[a].astype(F32)
        mp[EDGE + y_hi * rows + a] = jnp.full(mp.shape[1:], on, F32)
        xs[a, EDGE : EDGE + cols, :] = fields[a].astype(F32) * on
    own = pl.ds(EDGE, rows)
    xb[0, own] = xs[...].astype(BF)
    mp[0:EDGE] = jnp.full((EDGE,) + mp.shape[1:], jnp.where(z > 0, 1.0, 0.0), F32)
    mp[EDGE + 2 * rows :] = jnp.full((EDGE,) + mp.shape[1:], jnp.where(z < lats // 2 - 1, 1.0, 0.0), F32)
    epack[0] = shifted(xb[0, own], 0, 2).reshape(rows * 8, width).astype(BF)
    epack[1] = shifted(xb[0, own], wide - 8, 6).reshape(rows * 8, width).astype(BF)

    heard = 5
    for i in range(chips):
        heard += count((lat, i * CORES + core)) + count(place_1(lat, i * CORES + core))
        heard += count((band_1, i * CORES + sector_1 % 2))
        heard += jnp.where(is_halo, count(place_1(beside, i * CORES + core)), 0)
    pl.semaphore_wait(barrier, heard)

    def mask_copy():
        both = mp.at[pl.ds(EDGE + y_hi * rows, rows)]
        return remote(both, both, m_sem.at[0], m_sem.at[1], (lat + 1 - 2 * y_hi, lon))

    def edge_copies():
        return [
            remote(epack.at[0], erecv.at[1], e_send.at[0], e_recv.at[1], (lat, left)),
            remote(epack.at[1], erecv.at[0], e_send.at[1], e_recv.at[0], (lat, right)),
        ]

    def row_copies(n):
        columns = (pl.ds(16, wide - 32), pl.ds(0, 16), pl.ds(wide - 16, 16))[n]
        top, bottom = xb.at[0, pl.ds(EDGE, EDGE), columns], xb.at[0, pl.ds(rows, EDGE), columns]
        above, below = xb.at[0, pl.ds(0, EDGE), columns], xb.at[0, pl.ds(EDGE + rows, EDGE), columns]
        return [
            remote(top, below, l_send.at[n, 0], l_recv.at[n, 1], (up, lon)),
            remote(bottom, above, l_send.at[n, 1], l_recv.at[n, 0], (down, lon)),
        ]

    for copy in edge_copies() + row_copies(0):
        copy.start()
    mask_copy().start()

    for copy in edge_copies():
        copy.wait_recv()
    with_edges(
        xb.at[0], own,
        erecv[0].astype(F32).reshape(rows, 8, width), erecv[1].astype(F32).reshape(rows, 8, width),
    )
    for copy in row_copies(1) + row_copies(2):
        copy.start()

    def row_mask(first, count):
        on = mp[pl.ds(first, count)][:, :1, :]
        return jnp.concatenate([on, on], axis=2)

    def norm(cells, blk):
        mean_of = jnp.full((width, width), 1.0 / width, BF)
        off = cells.astype(F32) - jnp.dot(cells, mean_of, preferred_element_type=F32)
        var = jnp.dot((off * off).astype(BF), mean_of, preferred_element_type=F32)
        return (off * lax.rsqrt(var + 1e-05) * gain[pl.ds(blk, 1)]).astype(BF)

    column = lax.broadcasted_iota(jnp.int32, (1, wide, 1), 1)
    inside = (column >= EDGE) & (column < EDGE + cols)

    def block(blk):
        x = xb.at[blk]
        w1_copy, w2_copy, wqkv_copy, wo_copy = weight_copies(blk)
        band = lat + blk * (band_1 - lat)
        sector = lon + blk * (sector_1 - lon)
        parity = sector % 2
        first_row = band % 2 * rows

        def arrived(place):
            source = row_at(place)

            @pl.when(elsewhere(source))
            def _():
                state_copy(att.at[0, 0], 1, place, h_send.at[0, 0], (lat, sibling)).wait_recv()

        def state_copy(src, to_blk, place, send, to):
            return remote(src, xb.at[to_blk, place], send, x_recv.at[to_blk, place], to)

        w1_copy.wait()

        @pl.when(blk == 1)
        def _():
            each(rows, lambda r: arrived(EDGE + r))

        def first(start):
            got = conv(x, start, EDGE, 1, w1.at[blk])
            got = jax.nn.gelu(got).reshape(EDGE, wide, width) * row_mask(first_row + start + 1, EDGE)
            hb[pl.ds(start, EDGE)] = got.astype(BF)

        each(2, lambda k: first(EDGE * (1 + k)))

        @pl.when(blk == 0)
        def _():
            for n in range(3):
                for copy in row_copies(n):
                    copy.wait_recv()
            mask_copy().wait_recv()

        @pl.when(blk == 1)
        def _():
            each(EDGE, arrived)
            each(EDGE, lambda r: arrived(EDGE + rows + r))

        @pl.when(band == 0)
        def _():
            x[0:EDGE] = jnp.zeros((EDGE, wide, width), BF)

        @pl.when(band == lats - 1)
        def _():
            x[EDGE + rows :] = jnp.zeros((EDGE, wide, width), BF)

        each(2, lambda k: first(3 * EDGE * k))

        w2_copy.wait()

        def row_copy(r):
            return remote(
                nself.at[blk, r], nbuf.at[blk, parity, sector // 2], f_send.at[blk, r],
                f_recv.at[blk, sector // 2], (band, r * CORES + parity),
            )

        def second(k):
            a = across(k) * 2
            got = jax.nn.gelu(conv(hb, a, 2, 2, w2.at[blk])).reshape(2, wide, width)
            got = (x[pl.ds(a + EDGE, 2)].astype(F32) + got) * row_mask(first_row + a + EDGE, 2)
            nself[blk, pl.ds(a, 2)] = got.astype(BF)
            for i in range(2):
                r = a + i
                far = elsewhere((band, r * CORES + parity))

                @pl.when(far)
                def _():
                    row_copy(r).start()

                @pl.when(jnp.logical_not(far))
                def _():
                    nbuf[blk, parity, sector // 2] = nself[blk, r]

        each(groups, second)

        def half_copy(i):
            slot = nbuf.at[blk, core, i]
            return remote(slot, slot, s_send.at[blk, i], s_recv.at[blk, i], (lat, sibling))

        def pass_on(k):
            i = across(k // 2) * 2 + k % 2

            @pl.when(elsewhere(placed(blk, lat, i * CORES + core)))
            def _():
                remote(
                    nself.at[blk, i], nbuf.at[blk, core, i], f_send.at[blk, i], f_recv.at[blk, i],
                    (lat, sibling),
                ).wait_recv()

            half_copy(i).start()

        each(chips, pass_on)

        wqkv_copy.wait()
        first_head = lax.broadcasted_iota(jnp.int32, (1, 1, 2 * head_dim), 2) < head_dim
        ones = jnp.where(inside, 1.0, 0.0)

        def keys_values(t):
            side = (core + t) % CORES

            @pl.when(t == 1)
            def _():
                each(chips, lambda i: half_copy(i).wait_recv())

            cells = norm(nbuf[blk, side].reshape(half, width), blk)
            cells = jnp.where(inside, cells.reshape(chips, wide, width), jnp.zeros((), BF))
            cells = cells.reshape(half, width)
            both = jnp.dot(cells, wqkv[blk, :, width:], preferred_element_type=F32)
            kb[side] = both[:, :width].astype(BF).reshape(chips, wide, width)
            values = both[:, width:].reshape(chips, wide, width)
            for h in range(HEADS):
                pair = values[:, :, h // 2 * 2 * head_dim :][:, :, : 2 * head_dim]
                keep = first_head if h % 2 == 0 else ~first_head
                vx[h, side] = jnp.where(keep, pair, ones).astype(BF)

        each(CORES, keys_values)

        qm[...] = nbuf[blk, core]

        def join(i):
            before, after = (i + chips - 1 + core) % chips, (i + core) % chips
            from_left = shifted(nbuf[blk, 1 - core, pl.ds(before, 1)], wide - 8, 6)
            from_right = shifted(nbuf[blk, 1 - core, pl.ds(after, 1)], 0, 2)
            with_edges(qm, pl.ds(i, 1), from_left, from_right)

        each(chips, join)
        wo_copy.wait()

        def home_copy(i):
            to = placed(1 - blk, lat, i * CORES + core)
            return to, state_copy(att.at[blk, i], blk + 1, EDGE + chip, h_send.at[blk, i], to)

        beside_at = chip - (rows - EDGE) + (7 - chip) // 5 * 16

        def halo_copy(i):
            to = place_1(beside, i * CORES + core)
            return to, state_copy(att.at[0, i], 1, beside_at, n_send.at[i], to)

        def attend(k):
            a = across(k) * 2
            cells = qm[pl.ds(a, 2)].reshape(2 * wide, width)
            scale = math.log2(math.e) / math.sqrt(head_dim)
            query = jnp.dot(norm(cells, blk), wqkv[blk, :, :width], preferred_element_type=F32)
            query = (query * scale).astype(BF)
            low_lane = lax.broadcasted_iota(jnp.int32, (1, 2 * head_dim), 1) < head_dim
            zero = jnp.zeros((), BF)
            attended = []
            for p in range(HEADS // 2):
                span = slice(p * 2 * head_dim, (p + 1) * 2 * head_dim)
                both = query[:, span]
                lhs = jnp.concatenate(
                    [jnp.where(low_lane, both, zero), jnp.where(low_lane, zero, both)], axis=0
                )
                keys = kb[:, :, :, span].reshape(CORES * half, 2 * head_dim)
                scores = lax.dot_general(
                    lhs, keys, (((1,), (1,)), ((), ())), preferred_element_type=F32
                )
                expo = jnp.exp2(scores).astype(BF)
                got = []
                for e in range(2):
                    values = vx[2 * p + e].reshape(CORES * half, 2 * head_dim)
                    part = jnp.dot(
                        expo[e * 2 * wide : (e + 1) * 2 * wide], values, preferred_element_type=F32
                    )
                    got.append(part / pltpu.roll(part, head_dim, 1))
                attended.append(jnp.where(low_lane, got[0], got[1]).astype(BF))
            update = jnp.dot(
                jnp.concatenate(attended, axis=1), wo[blk], preferred_element_type=F32
            )
            state = (cells.astype(F32) + update).reshape(2, wide, width) * row_mask(EDGE + y_hi * rows + chip, 1)
            att[blk, pl.ds(a, 2)] = state.astype(BF)
            for n in range(2):
                i = a + n
                to, copy = home_copy(i)
                far = elsewhere(to)

                @pl.when(far)
                def _():
                    copy.start()

                @pl.when(jnp.logical_not(far))
                def _():
                    xb[blk + 1, EDGE + chip] = att[blk, i]

                @pl.when((blk == 0) & is_halo)
                def _():
                    to, copy = halo_copy(i)
                    far = elsewhere(to)

                    @pl.when(far)
                    def _():
                        copy.start()

                    @pl.when(jnp.logical_not(far))
                    def _():
                        xb[1, beside_at] = att[0, i]

        each(groups, attend)

        def left_here(i):
            @pl.when(elsewhere((band, i * CORES + parity)))
            def _():
                row_copy(i).wait_send()

            half_copy(i).wait_send()
            to, copy = home_copy(i)

            @pl.when(elsewhere(to))
            def _():
                copy.wait_send()

            @pl.when((blk == 0) & is_halo)
            def _():
                to, copy = halo_copy(i)

                @pl.when(elsewhere(to))
                def _():
                    copy.wait_send()

        each(chips, left_here)

    each(BLOCKS, block)

    for copy in edge_copies() + row_copies(0) + row_copies(1) + row_copies(2) + [mask_copy()]:
        copy.wait_send()

    def come_home(r):
        @pl.when(r != chip)
        def _():
            remote(
                att.at[0, 0], xb.at[BLOCKS, EDGE + r], h_send.at[0, 0], x_recv.at[BLOCKS, EDGE + r],
                (lat, sibling),
            ).wait_recv()

    each(rows, come_home)
    out[...] = xb[BLOCKS, own]


def body(fields, lat_mask, conv_first, conv_second, norm_gain, qkv_weight, out_weight):
    rows, cols, width = fields.shape
    wide = cols + 2 * EDGE
    chips = lax.axis_size("lon") // CORES
    head_dim = width // HEADS
    vmem = pl.BlockSpec(memory_space=pltpu.VMEM)
    hbm = pl.BlockSpec(memory_space=pl.ANY)
    dma = pltpu.SemaphoreType.DMA
    wide_out = pl.pallas_call(
        kernel,
        out_shape=jax.ShapeDtypeStruct((rows, wide, width), BF),
        in_specs=[vmem, pl.BlockSpec(memory_space=pltpu.SMEM), hbm, hbm, vmem, hbm, hbm],
        out_specs=vmem,
        scratch_shapes=[
            pltpu.VMEM(conv_first.shape, BF),
            pltpu.VMEM(conv_second.shape, BF),
            pltpu.VMEM(qkv_weight.shape, BF),
            pltpu.VMEM(out_weight.shape, BF),
            pltpu.VMEM((rows, wide, width), F32),
            pltpu.VMEM((BLOCKS + 1, rows + 2 * EDGE, wide, width), BF),
            pltpu.VMEM((rows + 4, wide, width), BF),
            pltpu.VMEM((2 * rows + 2 * EDGE, 8, width // 2), F32),
            pltpu.VMEM((2, rows * 8, width), BF),
            pltpu.VMEM((2, rows * 8, width), BF),
            pltpu.VMEM((BLOCKS, rows, wide, width), BF),
            pltpu.VMEM((BLOCKS, CORES, chips, wide, width), BF),
            pltpu.VMEM((chips, wide, width), BF),
            pltpu.VMEM((CORES, chips, wide, width), BF),
            pltpu.VMEM((HEADS, CORES, chips, wide, 2 * head_dim), BF),
            pltpu.VMEM((BLOCKS, chips, wide, width), BF),
            dma((4, BLOCKS)),
            dma((2,)),
            dma((2,)),
            dma((3, 2)),
            dma((3, 2)),
            dma((2,)),
            dma((BLOCKS, rows)),
            dma((BLOCKS, chips)),
            dma((BLOCKS, chips)),
            dma((BLOCKS, chips)),
            dma((BLOCKS, chips)),
            dma((chips,)),
            dma((BLOCKS + 1, rows + 2 * EDGE)),
        ],
        compiler_params=pltpu.CompilerParams(
            collective_id=0, has_side_effects=True, vmem_limit_bytes=60 * 1024 * 1024
        ),
    )(fields, lat_mask, conv_first, conv_second, norm_gain, qkv_weight, out_weight)
    return wide_out[:, EDGE : EDGE + cols]


def solution(mesh):
    placed = (P("lat", "lon", None), P("lat"), P(), P(), P(), P(), P())
    return jax.shard_map(
        body, mesh=mesh, in_specs=placed, out_specs=P("lat", "lon", None), check_vma=False
    )
```

```python
import math

import jax
import jax.numpy as jnp
from jax import lax
from jax.experimental import pallas as pl
from jax.experimental.pallas import tpu as pltpu
from jax.sharding import PartitionSpec as P

HEADS = 4
BLOCKS = 2
EDGE = 3
CORES = 2
RING = 4
BF = jnp.bfloat16
F32 = jnp.float32
MESH = pl.DeviceIdType.MESH


def conv(src, start, count, spread, weights):
    wide, width = src.shape[1], src.shape[2]
    cells = count * wide
    taps = [src[pl.ds(start + i * spread, count)].reshape(cells, width) for i in range(3)]
    lhs = jnp.concatenate(taps, axis=1)
    parts = [
        jnp.dot(lhs, weights[:, j].reshape(3 * width, width), preferred_element_type=F32)
        for j in range(3)
    ]
    return pltpu.roll(parts[0], spread, 0) + parts[1] + pltpu.roll(parts[2], cells - spread, 0)


def shifted(cells, start, by):
    tile = cells[:, start // 16 * 16 : start // 16 * 16 + 16, :].astype(F32)
    return pltpu.roll(tile[:, start % 16 : start % 16 + 8], by, 1)


def with_edges(ref, index, from_left, from_right):
    count, _, width = from_left.shape
    wide = ref.shape[-2]
    place = lax.broadcasted_iota(jnp.int32, (count, 16, width), 1)
    nothing = jnp.zeros(from_left.shape, F32)
    low = ref[index, 0:16, :].astype(F32)
    high = ref[index, wide - 16 : wide, :].astype(F32)
    ref[index, 0:16, :] = jnp.where(
        place < EDGE, jnp.concatenate([from_left, nothing], axis=1), low
    ).astype(BF)
    ref[index, wide - 16 : wide, :] = jnp.where(
        place >= 16 - EDGE, jnp.concatenate([nothing, from_right], axis=1), high
    ).astype(BF)


def kernel(
    fields, mask, w1_hbm, w2_hbm, gain, wqkv_hbm, wo_hbm, out,
    w1, w2, wqkv, wo, xs, xb, hb, mp, epack, erecv, nself, nbuf, qm, qb, kb, vx, att,
    wsem, e_send, e_recv, l_send, l_recv, m_sem, f_send, f_recv, s_send, s_recv, h_send, x_recv,
):
    cols, rows, width = fields.shape
    wide = cols + 2 * EDGE
    head_dim = width // HEADS
    lats, lons = lax.axis_size("lat"), lax.axis_size("lon")
    chips = lons // CORES
    groups = chips // 2
    half = chips * wide
    lat, lon = lax.axis_index("lat"), lax.axis_index("lon")
    chip, core = lon // CORES, lon % CORES
    z, y_hi = lat // 2, lat % 2
    x_at, y_at = lon // 4, y_hi * 2 + (lon // 2) % 2
    up, down = (lat + lats - 1) % lats, (lat + 1) % lats
    left, right = (lon + lons - 1) % lons, (lon + 1) % lons
    sibling = chip * CORES + 1 - core
    band_1, sector_1 = z * 2 + core, x_at * 4 + (y_at + x_at) % RING

    def place_1(band, sector):
        x = sector // 4
        y = (sector + 3 * x) % RING
        return band // 2 * 2 + y // 2, x * 4 + y % 2 * 2 + band % 2

    def placed(blk, band, sector):
        there = place_1(band, sector)
        return band + blk * (there[0] - band), sector + blk * (there[1] - sector)

    def elsewhere(to):
        return (to[0] != lat) | (to[1] != lon)

    def remote(src, dst, send, recv, to):
        return pltpu.make_async_remote_copy(
            src_ref=src, dst_ref=dst, send_sem=send, recv_sem=recv, device_id=to, device_id_type=MESH
        )

    def each(count, body):
        lax.fori_loop(0, count, lambda k, carry: (body(k), carry)[1], 0)

    def across(k):
        return (x_at + 2 - k + k // 2 * (2 * k - 1) + RING) % RING

    barrier = pltpu.get_barrier_semaphore()

    def greet(to):
        @pl.when(elsewhere(to))
        def _():
            pl.semaphore_signal(barrier, inc=1, device_id=to, device_id_type=MESH)

    def count(to):
        return jnp.where(elsewhere(to), 1, 0)

    up_1 = place_1((band_1 + lats - 1) % lats, sector_1)
    down_1 = place_1((band_1 + 1) % lats, sector_1)

    for to in ((up, lon), (down, lon), (lat, left), (lat, right), (lat, sibling), up_1, down_1):
        greet(to)
    each(chips, lambda i: greet((lat, i * CORES + core)))
    each(chips, lambda i: greet(place_1(lat, i * CORES + core)))
    each(rows, lambda r: greet((band_1, r * CORES + sector_1 % 2)))

    def weight_copies(blk):
        return [
            pltpu.make_async_copy(w1_hbm.at[blk], w1.at[blk], wsem.at[0, blk]),
            pltpu.make_async_copy(w2_hbm.at[blk], w2.at[blk], wsem.at[1, blk]),
            pltpu.make_async_copy(wqkv_hbm.at[blk], wqkv.at[blk], wsem.at[2, blk]),
            pltpu.make_async_copy(wo_hbm.at[blk], wo.at[blk], wsem.at[3, blk]),
        ]

    for blk in range(BLOCKS):
        for copy in weight_copies(blk):
            copy.start()

    xs[0:EDGE] = jnp.zeros((EDGE, rows, width), F32)
    xs[EDGE + cols :] = jnp.zeros((EDGE, rows, width), F32)
    xs[EDGE : EDGE + cols] = fields[...].astype(F32)
    own = pl.ds(EDGE, rows)
    for a in range(rows):
        on = mask[a].astype(F32)
        mp[EDGE + y_hi * rows + a] = jnp.full(mp.shape[1:], on, F32)
        xb[0, EDGE + a] = (xs[:, a, :] * on).astype(BF)
    mp[0:EDGE] = jnp.full((EDGE,) + mp.shape[1:], jnp.where(z > 0, 1.0, 0.0), F32)
    mp[EDGE + 2 * rows :] = jnp.full((EDGE,) + mp.shape[1:], jnp.where(z < lats // 2 - 1, 1.0, 0.0), F32)
    epack[0] = shifted(xb[0, own], 0, 2).reshape(rows * 8, width).astype(BF)
    epack[1] = shifted(xb[0, own], wide - 8, 6).reshape(rows * 8, width).astype(BF)

    heard = 7
    for i in range(chips):
        heard += count((lat, i * CORES + core)) + count(place_1(lat, i * CORES + core))
        heard += count((band_1, i * CORES + sector_1 % 2))
    pl.semaphore_wait(barrier, heard)

    def mask_copy():
        both = mp.at[pl.ds(EDGE + y_hi * rows, rows)]
        return remote(both, both, m_sem.at[0], m_sem.at[1], (lat + 1 - 2 * y_hi, lon))

    def edge_copies():
        return [
            remote(epack.at[0], erecv.at[1], e_send.at[0], e_recv.at[1], (lat, left)),
            remote(epack.at[1], erecv.at[0], e_send.at[1], e_recv.at[0], (lat, right)),
        ]

    def row_copies(n):
        blk, to_up, to_down = (1, up_1, down_1) if n == 3 else (0, (up, lon), (down, lon))
        columns = (pl.ds(16, wide - 32), pl.ds(0, 16), pl.ds(wide - 16, 16), pl.ds(0, wide))[n]
        top, bottom = xb.at[blk, pl.ds(EDGE, EDGE), columns], xb.at[blk, pl.ds(rows, EDGE), columns]
        above, below = xb.at[blk, pl.ds(0, EDGE), columns], xb.at[blk, pl.ds(EDGE + rows, EDGE), columns]
        return [
            remote(top, below, l_send.at[n, 0], l_recv.at[n, 1], to_up),
            remote(bottom, above, l_send.at[n, 1], l_recv.at[n, 0], to_down),
        ]

    for copy in edge_copies() + row_copies(0):
        copy.start()
    mask_copy().start()

    for copy in edge_copies():
        copy.wait_recv()
    with_edges(
        xb.at[0], own,
        erecv[0].astype(F32).reshape(rows, 8, width), erecv[1].astype(F32).reshape(rows, 8, width),
    )
    for copy in row_copies(1) + row_copies(2):
        copy.start()

    def row_mask(first, count):
        on = mp[pl.ds(first, count)][:, :1, :]
        return jnp.concatenate([on, on], axis=2)

    def norm(cells, blk):
        mean_of = jnp.full((width, width), 1.0 / width, BF)
        off = cells.astype(F32) - jnp.dot(cells, mean_of, preferred_element_type=F32)
        var = jnp.dot((off * off).astype(BF), mean_of, preferred_element_type=F32)
        return (off * lax.rsqrt(var + 1e-05) * gain[pl.ds(blk, 1)]).astype(BF)

    column = lax.broadcasted_iota(jnp.int32, (1, wide, 1), 1)
    inside = (column >= EDGE) & (column < EDGE + cols)

    def state_copy(blk, i, to_blk, r, to):
        return remote(
            att.at[blk, i], xb.at[to_blk, EDGE + r], h_send.at[blk, i], x_recv.at[to_blk, r], to
        )

    def block(blk):
        x = xb.at[blk]
        w1_copy, w2_copy, wqkv_copy, wo_copy = weight_copies(blk)
        band = lat + blk * (band_1 - lat)
        sector = lon + blk * (sector_1 - lon)
        parity = sector % 2
        first_row = band % 2 * rows

        def arrived(r):
            @pl.when(elsewhere((band_1, r * CORES + sector_1 % 2)))
            def _():
                state_copy(0, 0, 1, r, (lat, sibling)).wait_recv()

        w1_copy.wait()

        @pl.when(blk == 1)
        def _():
            to_up, to_down = row_copies(3)
            each(EDGE, arrived)
            to_up.start()
            each(EDGE, lambda r: arrived(rows - EDGE + r))
            to_down.start()
            each(rows - 2 * EDGE, lambda r: arrived(EDGE + r))

        def first(start):
            got = conv(x, start, EDGE, 1, w1.at[blk])
            got = jax.nn.gelu(got).reshape(EDGE, wide, width) * row_mask(first_row + start + 1, EDGE)
            hb[pl.ds(start, EDGE)] = got.astype(BF)

        each(2, lambda k: first(EDGE * (1 + k)))

        @pl.when(blk == 0)
        def _():
            for n in range(3):
                for copy in row_copies(n):
                    copy.wait_recv()
            mask_copy().wait_recv()

        @pl.when(blk == 1)
        def _():
            for copy in row_copies(3):
                copy.wait_recv()

        @pl.when(band == 0)
        def _():
            x[0:EDGE] = jnp.zeros((EDGE, wide, width), BF)

        @pl.when(band == lats - 1)
        def _():
            x[EDGE + rows :] = jnp.zeros((EDGE, wide, width), BF)

        each(2, lambda k: first(3 * EDGE * k))

        w2_copy.wait()

        def row_copy(r):
            return remote(
                nself.at[blk, r], nbuf.at[blk, parity, sector // 2], f_send.at[blk, r],
                f_recv.at[blk, sector // 2], (band, r * CORES + parity),
            )

        def second(k):
            a = across(k) * 2
            got = jax.nn.gelu(conv(hb, a, 2, 2, w2.at[blk])).reshape(2, wide, width)
            got = (x[pl.ds(a + EDGE, 2)].astype(F32) + got) * row_mask(first_row + a + EDGE, 2)
            nself[blk, pl.ds(a, 2)] = got.astype(BF)
            for i in range(2):
                r = a + i
                far = elsewhere((band, r * CORES + parity))

                @pl.when(far)
                def _():
                    row_copy(r).start()

                @pl.when(jnp.logical_not(far))
                def _():
                    nbuf[blk, parity, sector // 2] = nself[blk, r]

        each(groups, second)

        def half_copy(i):
            slot = nbuf.at[blk, core, i]
            return remote(slot, slot, s_send.at[blk, i], s_recv.at[blk, i], (lat, sibling))

        def pass_on(k):
            i = across(k // 2) * 2 + k % 2

            @pl.when(elsewhere(placed(blk, lat, i * CORES + core)))
            def _():
                remote(
                    nself.at[blk, i], nbuf.at[blk, core, i], f_send.at[blk, i], f_recv.at[blk, i],
                    (lat, sibling),
                ).wait_recv()

            half_copy(i).start()

        each(chips, pass_on)

        wqkv_copy.wait()
        first_head = lax.broadcasted_iota(jnp.int32, (1, 1, 2 * head_dim), 2) < head_dim
        ones = jnp.where(inside, 1.0, 0.0)

        def keys_values(t):
            side = (core + t) % CORES

            @pl.when(t == 1)
            def _():
                each(chips, lambda i: half_copy(i).wait_recv())

            cells = norm(nbuf[blk, side].reshape(half, width), blk)
            cells = jnp.where(inside, cells.reshape(chips, wide, width), jnp.zeros((), BF))
            cells = cells.reshape(half, width)
            both = jnp.dot(cells, wqkv[blk, :, width:], preferred_element_type=F32)
            kb[side] = both[:, :width].astype(BF).reshape(chips, wide, width)
            values = both[:, width:].reshape(chips, wide, width)
            for h in range(HEADS):
                pair = values[:, :, h // 2 * 2 * head_dim :][:, :, : 2 * head_dim]
                keep = first_head if h % 2 == 0 else ~first_head
                vx[h, side] = jnp.where(keep, pair, ones).astype(BF)

        each(CORES, keys_values)

        qm[...] = nbuf[blk, core]

        def join(i):
            before, after = (i + chips - 1 + core) % chips, (i + core) % chips
            from_left = shifted(nbuf[blk, 1 - core, pl.ds(before, 1)], wide - 8, 6)
            from_right = shifted(nbuf[blk, 1 - core, pl.ds(after, 1)], 0, 2)
            with_edges(qm, pl.ds(i, 1), from_left, from_right)

        each(chips, join)
        wo_copy.wait()

        norm_all = norm(qm[...].reshape(half, width), blk)
        query = jnp.dot(norm_all, wqkv[blk, :, :width], preferred_element_type=F32)
        scale = math.log2(math.e) / math.sqrt(head_dim)
        qb[...] = (query * scale).astype(BF).reshape(chips, wide, width)

        def home_copy(i):
            to = placed(1 - blk, lat, i * CORES + core)
            return to, state_copy(blk, i, blk + 1, chip, to)

        def attend(k):
            a = across(k) * 2
            query = qb[pl.ds(a, 2)].reshape(2 * wide, width)
            low_lane = lax.broadcasted_iota(jnp.int32, (1, 2 * head_dim), 1) < head_dim
            zero = jnp.zeros((), BF)
            attended = []
            for p in range(HEADS // 2):
                span = slice(p * 2 * head_dim, (p + 1) * 2 * head_dim)
                both = query[:, span]
                lhs = jnp.concatenate(
                    [jnp.where(low_lane, both, zero), jnp.where(low_lane, zero, both)], axis=0
                )
                keys = kb[:, :, :, span].reshape(CORES * half, 2 * head_dim)
                scores = lax.dot_general(
                    lhs, keys, (((1,), (1,)), ((), ())), preferred_element_type=F32
                )
                expo = jnp.exp2(scores).astype(BF)
                got = []
                for e in range(2):
                    values = vx[2 * p + e].reshape(CORES * half, 2 * head_dim)
                    part = jnp.dot(
                        expo[e * 2 * wide : (e + 1) * 2 * wide], values, preferred_element_type=F32
                    )
                    got.append(part / pltpu.roll(part, head_dim, 1))
                attended.append(jnp.where(low_lane, got[0], got[1]).astype(BF))
            update = jnp.dot(
                jnp.concatenate(attended, axis=1), wo[blk], preferred_element_type=F32
            )
            state = qm[pl.ds(a, 2)].astype(F32) + update.reshape(2, wide, width)
            state = state * row_mask(EDGE + y_hi * rows + chip, 1)
            att[blk, pl.ds(a, 2)] = state.astype(BF)
            for n in range(2):
                i = a + n
                to, copy = home_copy(i)
                far = elsewhere(to)

                @pl.when(far)
                def _():
                    copy.start()

                @pl.when(jnp.logical_not(far))
                def _():
                    xb[blk + 1, EDGE + chip] = att[blk, i]

        each(groups, attend)

    each(BLOCKS, block)

    def sent(blk):
        band = lat + blk * (band_1 - lat)
        parity = (lon + blk * (sector_1 - lon)) % 2

        def one(i):
            @pl.when(elsewhere((band, i * CORES + parity)))
            def _():
                remote(
                    nself.at[blk, i], nbuf.at[blk, core, i], f_send.at[blk, i], f_recv.at[blk, i], (lat, sibling)
                ).wait_send()

            slot = nbuf.at[blk, core, i]
            remote(slot, slot, s_send.at[blk, i], s_recv.at[blk, i], (lat, sibling)).wait_send()

            @pl.when(elsewhere(placed(1 - blk, lat, i * CORES + core)))
            def _():
                state_copy(blk, i, blk + 1, chip, (lat, sibling)).wait_send()

        each(chips, one)

    each(BLOCKS, sent)

    for copy in edge_copies() + sum((row_copies(n) for n in range(4)), []) + [mask_copy()]:
        copy.wait_send()

    def come_home(r):
        @pl.when(r != chip)
        def _():
            state_copy(0, 0, BLOCKS, r, (lat, sibling)).wait_recv()

    each(rows, come_home)
    for a in range(rows):
        xs[:, a, :] = xb[BLOCKS, EDGE + a].astype(F32)
    out[...] = xs[EDGE : EDGE + cols].astype(BF)


def body(fields, lat_mask, conv_first, conv_second, norm_gain, qkv_weight, out_weight):
    rows, cols, width = fields.shape
    wide = cols + 2 * EDGE
    chips = lax.axis_size("lon") // CORES
    head_dim = width // HEADS
    vmem = pl.BlockSpec(memory_space=pltpu.VMEM)
    hbm = pl.BlockSpec(memory_space=pl.ANY)
    dma = pltpu.SemaphoreType.DMA
    out = pl.pallas_call(
        kernel,
        out_shape=jax.ShapeDtypeStruct((cols, rows, width), BF),
        in_specs=[vmem, pl.BlockSpec(memory_space=pltpu.SMEM), hbm, hbm, vmem, hbm, hbm],
        out_specs=vmem,
        scratch_shapes=[
            pltpu.VMEM(conv_first.shape, BF),
            pltpu.VMEM(conv_second.shape, BF),
            pltpu.VMEM(qkv_weight.shape, BF),
            pltpu.VMEM(out_weight.shape, BF),
            pltpu.VMEM((wide, rows, width), F32),
            pltpu.VMEM((BLOCKS + 1, rows + 2 * EDGE, wide, width), BF),
            pltpu.VMEM((rows + 4, wide, width), BF),
            pltpu.VMEM((2 * rows + 2 * EDGE, 8, width // 2), F32),
            pltpu.VMEM((2, rows * 8, width), BF),
            pltpu.VMEM((2, rows * 8, width), BF),
            pltpu.VMEM((BLOCKS, rows, wide, width), BF),
            pltpu.VMEM((BLOCKS, CORES, chips, wide, width), BF),
            pltpu.VMEM((chips, wide, width), BF),
            pltpu.VMEM((chips, wide, width), BF),
            pltpu.VMEM((CORES, chips, wide, width), BF),
            pltpu.VMEM((HEADS, CORES, chips, wide, 2 * head_dim), BF),
            pltpu.VMEM((BLOCKS, chips, wide, width), BF),
            dma((4, BLOCKS)),
            dma((2,)),
            dma((2,)),
            dma((4, 2)),
            dma((4, 2)),
            dma((2,)),
            dma((BLOCKS, rows)),
            dma((BLOCKS, chips)),
            dma((BLOCKS, chips)),
            dma((BLOCKS, chips)),
            dma((BLOCKS, chips)),
            dma((BLOCKS + 1, rows)),
        ],
        compiler_params=pltpu.CompilerParams(
            collective_id=0, has_side_effects=True, vmem_limit_bytes=60 * 1024 * 1024
        ),
    )(jnp.transpose(fields, (1, 0, 2)), lat_mask, conv_first, conv_second, norm_gain, qkv_weight, out_weight)
    return jnp.transpose(out, (1, 0, 2))


def solution(mesh):
    placed = (P("lat", "lon", None), P("lat"), P(), P(), P(), P(), P())
    return jax.shard_map(
        body, mesh=mesh, in_specs=placed, out_specs=P("lat", "lon", None), check_vma=False
    )
```

```python
import math

import jax
import jax.numpy as jnp
from jax import lax
from jax.experimental import pallas as pl
from jax.experimental.pallas import tpu as pltpu
from jax.sharding import PartitionSpec as P

HEADS = 4
BLOCKS = 2
EDGE = 3
CORES = 2
RING = 4
BF = jnp.bfloat16
F32 = jnp.float32
MESH = pl.DeviceIdType.MESH


def conv(src, start, count, spread, weights):
    wide, width = src.shape[1], src.shape[2]
    cells = count * wide
    taps = [src[pl.ds(start + i * spread, count)].reshape(cells, width) for i in range(3)]
    lhs = jnp.concatenate(taps, axis=1)
    parts = [
        jnp.dot(lhs, weights[:, j].reshape(3 * width, width), preferred_element_type=F32)
        for j in range(3)
    ]
    return pltpu.roll(parts[0], spread, 0) + parts[1] + pltpu.roll(parts[2], cells - spread, 0)


def shifted(cells, start, by):
    tile = cells[:, start // 16 * 16 : start // 16 * 16 + 16, :].astype(F32)
    return pltpu.roll(tile[:, start % 16 : start % 16 + 8], by, 1)


def with_edges(ref, index, from_left, from_right):
    count, _, width = from_left.shape
    wide = ref.shape[-2]
    place = lax.broadcasted_iota(jnp.int32, (count, 16, width), 1)
    nothing = jnp.zeros(from_left.shape, F32)
    low = ref[index, 0:16, :].astype(F32)
    high = ref[index, wide - 16 : wide, :].astype(F32)
    ref[index, 0:16, :] = jnp.where(
        place < EDGE, jnp.concatenate([from_left, nothing], axis=1), low
    ).astype(BF)
    ref[index, wide - 16 : wide, :] = jnp.where(
        place >= 16 - EDGE, jnp.concatenate([nothing, from_right], axis=1), high
    ).astype(BF)


def kernel(
    fields_hbm, mask_hbm, w1_hbm, w2_hbm, gain_hbm, wqkv_hbm, wo_hbm, out,
    fields, mask, gain, w1, w2, wqkv, wo, xs, xb, hb, mp, epack, erecv, nself, nbuf, qm, qb, kb, vx, att,
    isem, wsem, e_send, e_recv, l_send, l_recv, m_sem, f_send, f_recv, s_send, s_recv, h_send, x_recv,
):
    cols, rows, width = fields.shape
    wide = cols + 2 * EDGE
    head_dim = width // HEADS
    lats, lons = lax.axis_size("lat"), lax.axis_size("lon")
    chips = lons // CORES
    groups = chips // 2
    half = chips * wide
    lat, lon = lax.axis_index("lat"), lax.axis_index("lon")
    chip, core = lon // CORES, lon % CORES
    z, y_hi = lat // 2, lat % 2
    x_at, y_at = lon // 4, y_hi * 2 + (lon // 2) % 2
    up, down = (lat + lats - 1) % lats, (lat + 1) % lats
    left, right = (lon + lons - 1) % lons, (lon + 1) % lons
    sibling = chip * CORES + 1 - core
    band_1, sector_1 = z * 2 + core, x_at * 4 + (y_at + x_at) % RING

    def place_1(band, sector):
        x = sector // 4
        y = (sector + 3 * x) % RING
        return band // 2 * 2 + y // 2, x * 4 + y % 2 * 2 + band % 2

    def placed(blk, band, sector):
        there = place_1(band, sector)
        return band + blk * (there[0] - band), sector + blk * (there[1] - sector)

    def elsewhere(to):
        return (to[0] != lat) | (to[1] != lon)

    def remote(src, dst, send, recv, to):
        return pltpu.make_async_remote_copy(
            src_ref=src, dst_ref=dst, send_sem=send, recv_sem=recv, device_id=to, device_id_type=MESH
        )

    def each(count, body):
        lax.fori_loop(0, count, lambda k, carry: (body(k), carry)[1], 0)

    def across(k):
        return (x_at + 2 - k + k // 2 * (2 * k - 1) + RING) % RING

    barrier = pltpu.get_barrier_semaphore()

    def greet(to):
        @pl.when(elsewhere(to))
        def _():
            pl.semaphore_signal(barrier, inc=1, device_id=to, device_id_type=MESH)

    up_1 = place_1((band_1 + lats - 1) % lats, sector_1)
    down_1 = place_1((band_1 + 1) % lats, sector_1)

    inputs = [
        pltpu.make_async_copy(mask_hbm, mask, isem.at[0]),
        pltpu.make_async_copy(fields_hbm, fields, isem.at[1]),
        pltpu.make_async_copy(gain_hbm, gain, isem.at[2]),
    ]

    def weight_copies(blk):
        return [
            pltpu.make_async_copy(w1_hbm.at[blk], w1.at[blk], wsem.at[0, blk]),
            pltpu.make_async_copy(w2_hbm.at[blk], w2.at[blk], wsem.at[1, blk]),
            pltpu.make_async_copy(wqkv_hbm.at[blk], wqkv.at[blk], wsem.at[2, blk]),
            pltpu.make_async_copy(wo_hbm.at[blk], wo.at[blk], wsem.at[3, blk]),
        ]

    for copy in inputs:
        copy.start()
    for blk in range(BLOCKS):
        for copy in weight_copies(blk):
            copy.start()

    for to in ((up, lon), (down, lon), (lat, left), (lat, right), (lat, sibling)):
        greet(to)
    each(chips, lambda i: greet((lat, i * CORES + core)))

    for copy in inputs:
        copy.wait()
    xs[0:EDGE] = jnp.zeros((EDGE, rows, width), F32)
    xs[EDGE + cols :] = jnp.zeros((EDGE, rows, width), F32)
    xs[EDGE : EDGE + cols] = fields[...].astype(F32)
    own = pl.ds(EDGE, rows)
    for a in range(rows):
        on = mask[a].astype(F32)
        mp[EDGE + y_hi * rows + a] = jnp.full(mp.shape[1:], on, F32)
        xb[0, EDGE + a] = (xs[:, a, :] * on).astype(BF)
    mp[0:EDGE] = jnp.full((EDGE,) + mp.shape[1:], jnp.where(z > 0, 1.0, 0.0), F32)
    mp[EDGE + 2 * rows :] = jnp.full((EDGE,) + mp.shape[1:], jnp.where(z < lats // 2 - 1, 1.0, 0.0), F32)
    epack[0] = shifted(xb[0, own], 0, 2).reshape(rows * 8, width).astype(BF)
    epack[1] = shifted(xb[0, own], wide - 8, 6).reshape(rows * 8, width).astype(BF)

    pl.semaphore_wait(barrier, 5 + chips - 1)

    def mask_copy():
        both = mp.at[pl.ds(EDGE + y_hi * rows, rows)]
        return remote(both, both, m_sem.at[0], m_sem.at[1], (lat + 1 - 2 * y_hi, lon))

    def edge_copies():
        return [
            remote(epack.at[0], erecv.at[1], e_send.at[0], e_recv.at[1], (lat, left)),
            remote(epack.at[1], erecv.at[0], e_send.at[1], e_recv.at[0], (lat, right)),
        ]

    def row_copies(n):
        blk, to_up, to_down = (1, up_1, down_1) if n == 3 else (0, (up, lon), (down, lon))
        columns = (pl.ds(16, wide - 32), pl.ds(0, 16), pl.ds(wide - 16, 16), pl.ds(0, wide))[n]
        top, bottom = xb.at[blk, pl.ds(EDGE, EDGE), columns], xb.at[blk, pl.ds(rows, EDGE), columns]
        above, below = xb.at[blk, pl.ds(0, EDGE), columns], xb.at[blk, pl.ds(EDGE + rows, EDGE), columns]
        return [
            remote(top, below, l_send.at[n, 0], l_recv.at[n, 1], to_up),
            remote(bottom, above, l_send.at[n, 1], l_recv.at[n, 0], to_down),
        ]

    for copy in edge_copies() + row_copies(0):
        copy.start()
    mask_copy().start()

    for copy in edge_copies():
        copy.wait_recv()
    with_edges(
        xb.at[0], own,
        erecv[0].astype(F32).reshape(rows, 8, width), erecv[1].astype(F32).reshape(rows, 8, width),
    )
    for copy in row_copies(1) + row_copies(2):
        copy.start()

    def row_mask(first, count):
        on = mp[pl.ds(first, count)][:, :1, :]
        return jnp.concatenate([on, on], axis=2)

    def norm(cells, blk):
        mean_of = jnp.full((width, width), 1.0 / width, BF)
        off = cells.astype(F32) - jnp.dot(cells, mean_of, preferred_element_type=F32)
        var = jnp.dot((off * off).astype(BF), mean_of, preferred_element_type=F32)
        return (off * lax.rsqrt(var + 1e-05) * gain[pl.ds(blk, 1)]).astype(BF)

    column = lax.broadcasted_iota(jnp.int32, (1, wide, 1), 1)
    inside = (column >= EDGE) & (column < EDGE + cols)

    def state_copy(blk, i, to_blk, r, to):
        return remote(
            att.at[blk, i], xb.at[to_blk, EDGE + r], h_send.at[blk, i], x_recv.at[to_blk, r], to
        )

    def block(blk):
        x = xb.at[blk]
        w1_copy, w2_copy, wqkv_copy, wo_copy = weight_copies(blk)
        band = lat + blk * (band_1 - lat)
        sector = lon + blk * (sector_1 - lon)
        parity = sector % 2
        first_row = band % 2 * rows

        def arrived(r):
            @pl.when(elsewhere((band_1, r * CORES + sector_1 % 2)))
            def _():
                state_copy(0, 0, 1, r, (lat, sibling)).wait_recv()

        w1_copy.wait()

        @pl.when(blk == 1)
        def _():
            to_up, to_down = row_copies(3)
            each(EDGE, arrived)
            to_up.start()
            each(EDGE, lambda r: arrived(rows - EDGE + r))
            to_down.start()
            each(rows - 2 * EDGE, lambda r: arrived(EDGE + r))

        def first(start):
            got = conv(x, start, EDGE, 1, w1.at[blk])
            got = jax.nn.gelu(got).reshape(EDGE, wide, width) * row_mask(first_row + start + 1, EDGE)
            hb[pl.ds(start, EDGE)] = got.astype(BF)

        each(2, lambda k: first(EDGE * (1 + k)))

        @pl.when(blk == 0)
        def _():
            for n in range(3):
                for copy in row_copies(n):
                    copy.wait_recv()
            mask_copy().wait_recv()

        @pl.when(blk == 1)
        def _():
            for copy in row_copies(3):
                copy.wait_recv()

        @pl.when(band == 0)
        def _():
            x[0:EDGE] = jnp.zeros((EDGE, wide, width), BF)

        @pl.when(band == lats - 1)
        def _():
            x[EDGE + rows :] = jnp.zeros((EDGE, wide, width), BF)

        w2_copy.wait()

        def row_copy(r):
            return remote(
                nself.at[blk, r], nbuf.at[blk, parity, sector // 2], f_send.at[blk, r],
                f_recv.at[blk, sector // 2], (band, r * CORES + parity),
            )

        def second(k):
            a = across(k) * 2

            @pl.when(k < 2)
            def _():
                first(3 * EDGE * ((across(0) // 2 + k) % 2))

            got = jax.nn.gelu(conv(hb, a, 2, 2, w2.at[blk])).reshape(2, wide, width)
            got = (x[pl.ds(a + EDGE, 2)].astype(F32) + got) * row_mask(first_row + a + EDGE, 2)
            nself[blk, pl.ds(a, 2)] = got.astype(BF)
            for i in range(2):
                r = a + i
                far = elsewhere((band, r * CORES + parity))

                @pl.when(far)
                def _():
                    row_copy(r).start()

                @pl.when(jnp.logical_not(far))
                def _():
                    nbuf[blk, parity, sector // 2] = nself[blk, r]

        each(groups, second)

        def half_copy(i):
            slot = nbuf.at[blk, core, i]
            return remote(slot, slot, s_send.at[blk, i], s_recv.at[blk, i], (lat, sibling))

        def pass_on(k):
            i = across(k // 2) * 2 + k % 2

            @pl.when(elsewhere(placed(blk, lat, i * CORES + core)))
            def _():
                remote(
                    nself.at[blk, i], nbuf.at[blk, core, i], f_send.at[blk, i], f_recv.at[blk, i],
                    (lat, sibling),
                ).wait_recv()

            half_copy(i).start()

        each(chips, pass_on)

        wqkv_copy.wait()
        first_head = lax.broadcasted_iota(jnp.int32, (1, 1, 2 * head_dim), 2) < head_dim
        ones = jnp.where(inside, 1.0, 0.0)

        scale = math.log2(math.e) / math.sqrt(head_dim)

        def set_query(cells):
            query = jnp.dot(cells, wqkv[blk, :, :width], preferred_element_type=F32)
            qb[...] = (query * scale).astype(BF).reshape(chips, wide, width)

        def keys_values(t):
            side = (core + t) % CORES

            @pl.when(t == 1)
            def _():
                each(chips, lambda i: half_copy(i).wait_recv())

            cells = norm(nbuf[blk, side].reshape(half, width), blk)

            @pl.when((t == 0) & (blk == BLOCKS - 1))
            def _():
                set_query(cells)

            cells = jnp.where(inside, cells.reshape(chips, wide, width), jnp.zeros((), BF))
            cells = cells.reshape(half, width)
            both = jnp.dot(cells, wqkv[blk, :, width:], preferred_element_type=F32)
            kb[side] = both[:, :width].astype(BF).reshape(chips, wide, width)
            values = both[:, width:].reshape(chips, wide, width)
            for h in range(HEADS):
                pair = values[:, :, h // 2 * 2 * head_dim :][:, :, : 2 * head_dim]
                keep = first_head if h % 2 == 0 else ~first_head
                vx[h, side] = jnp.where(keep, pair, ones).astype(BF).reshape(vx.shape[2:])

        qm[...] = nbuf[blk, core]
        each(CORES, keys_values)

        def join(i):
            before, after = (i + chips - 1 + core) % chips, (i + core) % chips
            from_left = shifted(nbuf[blk, 1 - core, pl.ds(before, 1)], wide - 8, 6)
            from_right = shifted(nbuf[blk, 1 - core, pl.ds(after, 1)], 0, 2)
            with_edges(qm, pl.ds(i, 1), from_left, from_right)

        @pl.when(blk < BLOCKS - 1)
        def _():
            each(chips, join)
            set_query(norm(qm[...].reshape(half, width), blk))

        wo_copy.wait()

        def home_copy(i):
            to = placed(1 - blk, lat, i * CORES + core)
            return to, state_copy(blk, i, blk + 1, chip, to)

        def attend(k):
            a = across(k) * 2
            query = qb[pl.ds(a, 2)].reshape(2 * wide, width)
            low_lane = lax.broadcasted_iota(jnp.int32, (1, 2 * head_dim), 1) < head_dim
            zero = jnp.zeros((), BF)
            attended = []
            for p in range(HEADS // 2):
                span = slice(p * 2 * head_dim, (p + 1) * 2 * head_dim)
                both = query[:, span]
                lhs = jnp.concatenate(
                    [jnp.where(low_lane, both, zero), jnp.where(low_lane, zero, both)], axis=0
                )
                keys = kb[:, :, :, span].reshape(CORES * half, 2 * head_dim)
                scores = lax.dot_general(
                    lhs, keys, (((1,), (1,)), ((), ())), preferred_element_type=F32
                )
                expo = jnp.exp2(scores).astype(BF)
                got = []
                for e in range(2):
                    values = vx[2 * p + e].reshape(CORES * half, 2 * head_dim)
                    part = jnp.dot(
                        expo[e * 2 * wide : (e + 1) * 2 * wide], values, preferred_element_type=F32
                    )
                    got.append(part / pltpu.roll(part, head_dim, 1))
                attended.append(jnp.where(low_lane, got[0], got[1]).astype(BF))
            update = jnp.dot(
                jnp.concatenate(attended, axis=1), wo[blk], preferred_element_type=F32
            )
            state = qm[pl.ds(a, 2)].astype(F32) + update.reshape(2, wide, width)
            state = state * row_mask(EDGE + y_hi * rows + chip, 1)
            att[blk, pl.ds(a, 2)] = state.astype(BF)
            for n in range(2):
                i = a + n
                to, copy = home_copy(i)
                far = elsewhere(to)

                @pl.when(far)
                def _():
                    copy.start()

                @pl.when(jnp.logical_not(far))
                def _():
                    xb[blk + 1, EDGE + chip] = att[blk, i]

        each(groups, attend)

    each(BLOCKS, block)

    def sent(blk):
        band = lat + blk * (band_1 - lat)
        parity = (lon + blk * (sector_1 - lon)) % 2

        def one(i):
            @pl.when(elsewhere((band, i * CORES + parity)))
            def _():
                remote(
                    nself.at[blk, i], nbuf.at[blk, core, i], f_send.at[blk, i], f_recv.at[blk, i], (lat, sibling)
                ).wait_send()

            slot = nbuf.at[blk, core, i]
            remote(slot, slot, s_send.at[blk, i], s_recv.at[blk, i], (lat, sibling)).wait_send()

            @pl.when(elsewhere(placed(1 - blk, lat, i * CORES + core)))
            def _():
                state_copy(blk, i, blk + 1, chip, (lat, sibling)).wait_send()

        each(chips, one)

    each(BLOCKS, sent)

    for copy in edge_copies() + sum((row_copies(n) for n in range(4)), []) + [mask_copy()]:
        copy.wait_send()

    def come_home(r):
        @pl.when(r != chip)
        def _():
            state_copy(0, 0, BLOCKS, r, (lat, sibling)).wait_recv()

    each(rows, come_home)
    out[...] = xb[BLOCKS, own]


def body(fields, lat_mask, conv_first, conv_second, norm_gain, qkv_weight, out_weight):
    rows, cols, width = fields.shape
    wide = cols + 2 * EDGE
    chips = lax.axis_size("lon") // CORES
    head_dim = width // HEADS
    vmem = pl.BlockSpec(memory_space=pltpu.VMEM)
    hbm = pl.BlockSpec(memory_space=pltpu.HBM)
    dma = pltpu.SemaphoreType.DMA
    wide_out = pl.pallas_call(
        kernel,
        out_shape=jax.ShapeDtypeStruct((rows, wide, width), BF),
        in_specs=[hbm] * 7,
        out_specs=vmem,
        scratch_shapes=[
            pltpu.VMEM((cols, rows, width), BF),
            pltpu.SMEM(lat_mask.shape, jnp.int32),
            pltpu.VMEM(norm_gain.shape, F32),
            pltpu.VMEM(conv_first.shape, BF),
            pltpu.VMEM(conv_second.shape, BF),
            pltpu.VMEM(qkv_weight.shape, BF),
            pltpu.VMEM(out_weight.shape, BF),
            pltpu.VMEM((wide, rows, width), F32),
            pltpu.VMEM((BLOCKS + 1, rows + 2 * EDGE, wide, width), BF),
            pltpu.VMEM((rows + 4, wide, width), BF),
            pltpu.VMEM((2 * rows + 2 * EDGE, 8, width // 2), F32),
            pltpu.VMEM((2, rows * 8, width), BF),
            pltpu.VMEM((2, rows * 8, width), BF),
            pltpu.VMEM((BLOCKS, rows, wide, width), BF),
            pltpu.VMEM((BLOCKS, CORES, chips, wide, width), BF),
            pltpu.VMEM((chips, wide, width), BF),
            pltpu.VMEM((chips, wide, width), BF),
            pltpu.VMEM((CORES, chips, wide, width), BF),
            pltpu.VMEM((HEADS, CORES, chips, wide, 2 * head_dim), BF),
            pltpu.VMEM((BLOCKS, chips, wide, width), BF),
            dma((3,)),
            dma((4, BLOCKS)),
            dma((2,)),
            dma((2,)),
            dma((4, 2)),
            dma((4, 2)),
            dma((2,)),
            dma((BLOCKS, rows)),
            dma((BLOCKS, chips)),
            dma((BLOCKS, chips)),
            dma((BLOCKS, chips)),
            dma((BLOCKS, chips)),
            dma((BLOCKS + 1, rows)),
        ],
        compiler_params=pltpu.CompilerParams(
            collective_id=0, has_side_effects=True, vmem_limit_bytes=60 * 1024 * 1024
        ),
    )(jnp.transpose(fields, (1, 0, 2)), lat_mask, conv_first, conv_second, norm_gain, qkv_weight, out_weight)
    return wide_out[:, EDGE : EDGE + cols]


def solution(mesh):
    placed = (P("lat", "lon", None), P("lat"), P(), P(), P(), P(), P())
    return jax.shard_map(
        body, mesh=mesh, in_specs=placed, out_specs=P("lat", "lon", None), check_vma=False
    )
```

```python
import math

import jax
import jax.numpy as jnp
from jax import lax
from jax.experimental import pallas as pl
from jax.experimental.pallas import tpu as pltpu
from jax.sharding import PartitionSpec as P

HEADS = 4
BLOCKS = 2
EDGE = 3
CORES = 2
RING = 4
BF = jnp.bfloat16
F32 = jnp.float32
MESH = pl.DeviceIdType.MESH


def conv(src, start, count, spread, weights):
    wide, width = src.shape[1], src.shape[2]
    cells = count * wide
    taps = [src[pl.ds(start + i * spread, count)].reshape(cells, width) for i in range(3)]
    lhs = jnp.concatenate(taps, axis=1)
    parts = [
        jnp.dot(lhs, weights[:, j].reshape(3 * width, width), preferred_element_type=F32)
        for j in range(3)
    ]
    return pltpu.roll(parts[0], spread, 0) + parts[1] + pltpu.roll(parts[2], cells - spread, 0)


def shifted(cells, start, by):
    tile = cells[:, start // 16 * 16 : start // 16 * 16 + 16, :].astype(F32)
    return pltpu.roll(tile[:, start % 16 : start % 16 + 8], by, 1)


def with_edges(ref, index, from_left, from_right):
    count, _, width = from_left.shape
    wide = ref.shape[-2]
    place = lax.broadcasted_iota(jnp.int32, (count, 16, width), 1)
    nothing = jnp.zeros(from_left.shape, F32)
    low = ref[index, 0:16, :].astype(F32)
    high = ref[index, wide - 16 : wide, :].astype(F32)
    ref[index, 0:16, :] = jnp.where(
        place < EDGE, jnp.concatenate([from_left, nothing], axis=1), low
    ).astype(BF)
    ref[index, wide - 16 : wide, :] = jnp.where(
        place >= 16 - EDGE, jnp.concatenate([nothing, from_right], axis=1), high
    ).astype(BF)


def kernel(
    fields_hbm, mask_hbm, w1_hbm, w2_hbm, gain_hbm, wqkv_hbm, wo_hbm, out,
    fields, mask, gain, w1, w2, wqkv, wo, xs, xb, hb, mp, epack, erecv, nself, nbuf, qm, qb, kb, vx, att,
    isem, wsem, e_send, e_recv, l_send, l_recv, m_sem, f_send, f_recv, s_send, s_recv, h_send, x_recv,
):
    cols, rows, width = fields.shape
    wide = cols + 2 * EDGE
    head_dim = width // HEADS
    lats, lons = lax.axis_size("lat"), lax.axis_size("lon")
    chips = lons // CORES
    groups = chips // 2
    half = chips * wide
    lat, lon = lax.axis_index("lat"), lax.axis_index("lon")
    chip, core = lon // CORES, lon % CORES
    z, y_hi = lat // 2, lat % 2
    x_at, y_at = lon // 4, y_hi * 2 + (lon // 2) % 2
    up, down = (lat + lats - 1) % lats, (lat + 1) % lats
    left, right = (lon + lons - 1) % lons, (lon + 1) % lons
    sibling = chip * CORES + 1 - core
    band_1, sector_1 = z * 2 + core, x_at * 4 + (y_at + x_at) % RING

    def place_1(band, sector):
        x = sector // 4
        y = (sector + 3 * x) % RING
        return band // 2 * 2 + y // 2, x * 4 + y % 2 * 2 + band % 2

    def placed(blk, band, sector):
        there = place_1(band, sector)
        return band + blk * (there[0] - band), sector + blk * (there[1] - sector)

    def elsewhere(to):
        return (to[0] != lat) | (to[1] != lon)

    def remote(src, dst, send, recv, to):
        return pltpu.make_async_remote_copy(
            src_ref=src, dst_ref=dst, send_sem=send, recv_sem=recv, device_id=to, device_id_type=MESH
        )

    def each(count, body):
        lax.fori_loop(0, count, lambda k, carry: (body(k), carry)[1], 0)

    def across(k):
        return (x_at + 2 - k + k // 2 * (2 * k - 1) + RING) % RING

    barrier = pltpu.get_barrier_semaphore()

    def greet(to):
        @pl.when(elsewhere(to))
        def _():
            pl.semaphore_signal(barrier, inc=1, device_id=to, device_id_type=MESH)

    up_1 = place_1((band_1 + lats - 1) % lats, sector_1)
    down_1 = place_1((band_1 + 1) % lats, sector_1)

    inputs = [
        pltpu.make_async_copy(mask_hbm, mask, isem.at[0]),
        pltpu.make_async_copy(fields_hbm, fields, isem.at[1]),
        pltpu.make_async_copy(gain_hbm, gain, isem.at[2]),
    ]

    def weight_copies(blk):
        return [
            pltpu.make_async_copy(w1_hbm.at[blk], w1.at[blk], wsem.at[0, blk]),
            pltpu.make_async_copy(w2_hbm.at[blk], w2.at[blk], wsem.at[1, blk]),
            pltpu.make_async_copy(wqkv_hbm.at[blk], wqkv.at[blk], wsem.at[2, blk]),
            pltpu.make_async_copy(wo_hbm.at[blk], wo.at[blk], wsem.at[3, blk]),
        ]

    for copy in inputs:
        copy.start()
    for blk in range(BLOCKS):
        for copy in weight_copies(blk):
            copy.start()

    for to in ((up, lon), (down, lon), (lat, left), (lat, right), (lat, sibling)):
        greet(to)
    each(chips, lambda i: greet((lat, i * CORES + core)))

    for copy in inputs:
        copy.wait()
    xs[0:EDGE] = jnp.zeros((EDGE, rows, width), F32)
    xs[EDGE + cols :] = jnp.zeros((EDGE, rows, width), F32)
    xs[EDGE : EDGE + cols] = fields[...].astype(F32)
    own = pl.ds(EDGE, rows)
    for a in range(rows):
        on = mask[a].astype(F32)
        mp[EDGE + y_hi * rows + a] = jnp.full(mp.shape[1:], on, F32)
        xb[0, EDGE + a] = (xs[:, a, :] * on).astype(BF)
    mp[0:EDGE] = jnp.full((EDGE,) + mp.shape[1:], jnp.where(z > 0, 1.0, 0.0), F32)
    mp[EDGE + 2 * rows :] = jnp.full((EDGE,) + mp.shape[1:], jnp.where(z < lats // 2 - 1, 1.0, 0.0), F32)
    epack[0] = shifted(xb[0, own], 0, 2).reshape(rows * 8, width).astype(BF)
    epack[1] = shifted(xb[0, own], wide - 8, 6).reshape(rows * 8, width).astype(BF)

    pl.semaphore_wait(barrier, 5 + chips - 1)

    def mask_copy():
        both = mp.at[pl.ds(EDGE + y_hi * rows, rows)]
        return remote(both, both, m_sem.at[0], m_sem.at[1], (lat + 1 - 2 * y_hi, lon))

    def edge_copies():
        return [
            remote(epack.at[0], erecv.at[1], e_send.at[0], e_recv.at[1], (lat, left)),
            remote(epack.at[1], erecv.at[0], e_send.at[1], e_recv.at[0], (lat, right)),
        ]

    def row_copies(n):
        blk, to_up, to_down = (1, up_1, down_1) if n == 3 else (0, (up, lon), (down, lon))
        columns = (pl.ds(16, wide - 32), pl.ds(0, 16), pl.ds(wide - 16, 16), pl.ds(0, wide))[n]
        top, bottom = xb.at[blk, pl.ds(EDGE, EDGE), columns], xb.at[blk, pl.ds(rows, EDGE), columns]
        above, below = xb.at[blk, pl.ds(0, EDGE), columns], xb.at[blk, pl.ds(EDGE + rows, EDGE), columns]
        return [
            remote(top, below, l_send.at[n, 0], l_recv.at[n, 1], to_up),
            remote(bottom, above, l_send.at[n, 1], l_recv.at[n, 0], to_down),
        ]

    for copy in edge_copies() + row_copies(0):
        copy.start()
    mask_copy().start()

    for copy in edge_copies():
        copy.wait_recv()
    with_edges(
        xb.at[0], own,
        erecv[0].astype(F32).reshape(rows, 8, width), erecv[1].astype(F32).reshape(rows, 8, width),
    )
    for copy in row_copies(1) + row_copies(2):
        copy.start()

    def row_mask(first, count):
        on = mp[pl.ds(first, count)][:, :1, :]
        return jnp.concatenate([on, on], axis=2)

    def norm(cells, blk):
        mean_of = jnp.full((width, width), 1.0 / width, BF)
        off = cells.astype(F32) - jnp.dot(cells, mean_of, preferred_element_type=F32)
        var = jnp.dot((off * off).astype(BF), mean_of, preferred_element_type=F32)
        return (off * lax.rsqrt(var + 1e-05) * gain[pl.ds(blk, 1)]).astype(BF)

    column = lax.broadcasted_iota(jnp.int32, (1, wide, 1), 1)
    inside = (column >= EDGE) & (column < EDGE + cols)

    def state_copy(blk, i, to_blk, r, to):
        return remote(
            att.at[blk, i], xb.at[to_blk, EDGE + r], h_send.at[blk, i], x_recv.at[to_blk, r], to
        )

    def block(blk):
        x = xb.at[blk]
        w1_copy, w2_copy, wqkv_copy, wo_copy = weight_copies(blk)
        band = lat + blk * (band_1 - lat)
        sector = lon + blk * (sector_1 - lon)
        parity = sector % 2
        first_row = band % 2 * rows

        def arrived(r):
            @pl.when(elsewhere((band_1, r * CORES + sector_1 % 2)))
            def _():
                state_copy(0, 0, 1, r, (lat, sibling)).wait_recv()

        w1_copy.wait()

        @pl.when(blk == 1)
        def _():
            to_up, to_down = row_copies(3)
            each(EDGE, arrived)
            to_up.start()
            each(EDGE, lambda r: arrived(rows - EDGE + r))
            to_down.start()
            each(rows - 2 * EDGE, lambda r: arrived(EDGE + r))

        def first(start):
            got = conv(x, start, EDGE, 1, w1.at[blk])
            got = jax.nn.gelu(got).reshape(EDGE, wide, width) * row_mask(first_row + start + 1, EDGE)
            hb[pl.ds(start, EDGE)] = got.astype(BF)

        each(2, lambda k: first(EDGE * (1 + k)))

        @pl.when(blk == 0)
        def _():
            for n in range(3):
                for copy in row_copies(n):
                    copy.wait_recv()
            mask_copy().wait_recv()

        @pl.when(blk == 1)
        def _():
            for copy in row_copies(3):
                copy.wait_recv()

        @pl.when(band == 0)
        def _():
            x[0:EDGE] = jnp.zeros((EDGE, wide, width), BF)

        @pl.when(band == lats - 1)
        def _():
            x[EDGE + rows :] = jnp.zeros((EDGE, wide, width), BF)

        w2_copy.wait()

        def row_copy(r):
            return remote(
                nself.at[blk, r], nbuf.at[blk, parity, sector // 2], f_send.at[blk, r],
                f_recv.at[blk, sector // 2], (band, r * CORES + parity),
            )

        def second(k):
            a = across(k) * 2

            @pl.when(k < 2)
            def _():
                first(3 * EDGE * ((across(0) // 2 + k) % 2))

            got = jax.nn.gelu(conv(hb, a, 2, 2, w2.at[blk])).reshape(2, wide, width)
            got = (x[pl.ds(a + EDGE, 2)].astype(F32) + got) * row_mask(first_row + a + EDGE, 2)
            nself[blk, pl.ds(a, 2)] = got.astype(BF)
            for i in range(2):
                r = a + i
                far = elsewhere((band, r * CORES + parity))

                @pl.when(far)
                def _():
                    row_copy(r).start()

                @pl.when(jnp.logical_not(far))
                def _():
                    nbuf[blk, parity, sector // 2] = nself[blk, r]

        each(groups, second)

        def half_copy(i):
            slot = nbuf.at[blk, core, i]
            return remote(slot, slot, s_send.at[blk, i], s_recv.at[blk, i], (lat, sibling))

        def pass_on(k):
            i = across(k // 2) * 2 + k % 2

            @pl.when(elsewhere(placed(blk, lat, i * CORES + core)))
            def _():
                remote(
                    nself.at[blk, i], nbuf.at[blk, core, i], f_send.at[blk, i], f_recv.at[blk, i],
                    (lat, sibling),
                ).wait_recv()

            half_copy(i).start()

        each(chips, pass_on)

        wqkv_copy.wait()
        first_head = lax.broadcasted_iota(jnp.int32, (1, 1, 2 * head_dim), 2) < head_dim
        ones = jnp.where(inside, 1.0, 0.0)

        scale = math.log2(math.e) / math.sqrt(head_dim)

        def set_query(cells):
            query = jnp.dot(cells, wqkv[blk, :, :width], preferred_element_type=F32)
            qb[...] = (query * scale).astype(BF).reshape(chips, wide, width)

        def keys_values(t):
            side = (core + t) % CORES

            @pl.when(t == 1)
            def _():
                each(chips, lambda i: half_copy(i).wait_recv())

            cells = norm(nbuf[blk, side].reshape(half, width), blk)

            @pl.when((t == 0) & (blk == BLOCKS - 1))
            def _():
                set_query(cells)

            cells = jnp.where(inside, cells.reshape(chips, wide, width), jnp.zeros((), BF))
            cells = cells.reshape(half, width)
            both = jnp.dot(cells, wqkv[blk, :, width:], preferred_element_type=F32)
            kb[side] = both[:, :width].astype(BF).reshape(chips, wide, width)
            values = both[:, width:].reshape(chips, wide, width)
            for h in range(HEADS):
                pair = values[:, :, h // 2 * 2 * head_dim :][:, :, : 2 * head_dim]
                keep = first_head if h % 2 == 0 else ~first_head
                vx[h, side] = jnp.where(keep, pair, ones).astype(BF).reshape(vx.shape[2:])

        qm[...] = nbuf[blk, core]
        each(CORES, keys_values)

        def join(i):
            before, after = (i + chips - 1 + core) % chips, (i + core) % chips
            from_left = shifted(nbuf[blk, 1 - core, pl.ds(before, 1)], wide - 8, 6)
            from_right = shifted(nbuf[blk, 1 - core, pl.ds(after, 1)], 0, 2)
            with_edges(qm, pl.ds(i, 1), from_left, from_right)

        @pl.when(blk < BLOCKS - 1)
        def _():
            each(chips, join)
            set_query(norm(qm[...].reshape(half, width), blk))

        wo_copy.wait()

        def home_copy(i):
            to = placed(1 - blk, lat, i * CORES + core)
            return to, state_copy(blk, i, blk + 1, chip, to)

        def attend(k):
            a = across(k) * 2
            query = qb[pl.ds(a, 2)].reshape(2 * wide, width)
            low_lane = lax.broadcasted_iota(jnp.int32, (1, 2 * head_dim), 1) < head_dim
            zero = jnp.zeros((), BF)
            attended = []
            for p in range(HEADS // 2):
                span = slice(p * 2 * head_dim, (p + 1) * 2 * head_dim)
                both = query[:, span]
                lhs = jnp.concatenate(
                    [jnp.where(low_lane, both, zero), jnp.where(low_lane, zero, both)], axis=0
                )
                keys = kb[:, :, :, span].reshape(CORES * half, 2 * head_dim)
                scores = lax.dot_general(
                    lhs, keys, (((1,), (1,)), ((), ())), preferred_element_type=F32
                )
                expo = jnp.exp2(scores).astype(BF)
                got = []
                for e in range(2):
                    values = vx[2 * p + e].reshape(CORES * half, 2 * head_dim)
                    part = jnp.dot(
                        expo[e * 2 * wide : (e + 1) * 2 * wide], values, preferred_element_type=F32
                    )
                    got.append(part / pltpu.roll(part, head_dim, 1))
                attended.append(jnp.where(low_lane, got[0], got[1]).astype(BF))
            update = jnp.dot(
                jnp.concatenate(attended, axis=1), wo[blk], preferred_element_type=F32
            )
            state = qm[pl.ds(a, 2)].astype(F32) + update.reshape(2, wide, width)
            state = state * row_mask(EDGE + y_hi * rows + chip, 1)
            att[blk, pl.ds(a, 2)] = state.astype(BF)
            for n in range(2):
                i = a + n
                to, copy = home_copy(i)
                far = elsewhere(to)

                @pl.when(far)
                def _():
                    copy.start()

                @pl.when(jnp.logical_not(far))
                def _():
                    xb[blk + 1, EDGE + chip] = att[blk, i]

        each(groups, attend)

    each(BLOCKS, block)

    def sent(blk):
        band = lat + blk * (band_1 - lat)
        parity = (lon + blk * (sector_1 - lon)) % 2

        def one(i):
            @pl.when(elsewhere((band, i * CORES + parity)))
            def _():
                remote(
                    nself.at[blk, i], nbuf.at[blk, core, i], f_send.at[blk, i], f_recv.at[blk, i], (lat, sibling)
                ).wait_send()

            slot = nbuf.at[blk, core, i]
            remote(slot, slot, s_send.at[blk, i], s_recv.at[blk, i], (lat, sibling)).wait_send()

            @pl.when(elsewhere(placed(1 - blk, lat, i * CORES + core)))
            def _():
                state_copy(blk, i, blk + 1, chip, (lat, sibling)).wait_send()

        each(chips, one)

    each(BLOCKS, sent)

    for copy in edge_copies() + sum((row_copies(n) for n in range(4)), []) + [mask_copy()]:
        copy.wait_send()

    def come_home(r):
        @pl.when(r != chip)
        def _():
            state_copy(0, 0, BLOCKS, r, (lat, sibling)).wait_recv()

    each(rows, come_home)
    out[...] = xb[BLOCKS, own]


def body(fields, lat_mask, conv_first, conv_second, norm_gain, qkv_weight, out_weight):
    rows, cols, width = fields.shape
    wide = cols + 2 * EDGE
    chips = lax.axis_size("lon") // CORES
    head_dim = width // HEADS
    vmem = pl.BlockSpec(memory_space=pltpu.VMEM)
    hbm = pl.BlockSpec(memory_space=pltpu.HBM)
    dma = pltpu.SemaphoreType.DMA
    wide_out = pl.pallas_call(
        kernel,
        out_shape=pltpu.VMEM((rows, wide, width), BF),
        in_specs=[hbm] * 7,
        out_specs=vmem,
        scratch_shapes=[
            pltpu.VMEM((cols, rows, width), BF),
            pltpu.SMEM(lat_mask.shape, jnp.int32),
            pltpu.VMEM(norm_gain.shape, F32),
            pltpu.VMEM(conv_first.shape, BF),
            pltpu.VMEM(conv_second.shape, BF),
            pltpu.VMEM(qkv_weight.shape, BF),
            pltpu.VMEM(out_weight.shape, BF),
            pltpu.VMEM((wide, rows, width), F32),
            pltpu.VMEM((BLOCKS + 1, rows + 2 * EDGE, wide, width), BF),
            pltpu.VMEM((rows + 4, wide, width), BF),
            pltpu.VMEM((2 * rows + 2 * EDGE, 8, width // 2), F32),
            pltpu.VMEM((2, rows * 8, width), BF),
            pltpu.VMEM((2, rows * 8, width), BF),
            pltpu.VMEM((BLOCKS, rows, wide, width), BF),
            pltpu.VMEM((BLOCKS, CORES, chips, wide, width), BF),
            pltpu.VMEM((chips, wide, width), BF),
            pltpu.VMEM((chips, wide, width), BF),
            pltpu.VMEM((CORES, chips, wide, width), BF),
            pltpu.VMEM((HEADS, CORES, chips, wide, 2 * head_dim), BF),
            pltpu.VMEM((BLOCKS, chips, wide, width), BF),
            dma((3,)),
            dma((4, BLOCKS)),
            dma((2,)),
            dma((2,)),
            dma((4, 2)),
            dma((4, 2)),
            dma((2,)),
            dma((BLOCKS, rows)),
            dma((BLOCKS, chips)),
            dma((BLOCKS, chips)),
            dma((BLOCKS, chips)),
            dma((BLOCKS, chips)),
            dma((BLOCKS + 1, rows)),
        ],
        compiler_params=pltpu.CompilerParams(
            collective_id=0, has_side_effects=True, vmem_limit_bytes=60 * 1024 * 1024
        ),
    )(jnp.transpose(fields, (1, 0, 2)), lat_mask, conv_first, conv_second, norm_gain, qkv_weight, out_weight)
    return wide_out[:, EDGE : EDGE + cols]


def solution(mesh):
    placed = (P("lat", "lon", None), P("lat"), P(), P(), P(), P(), P())
    return jax.shard_map(
        body, mesh=mesh, in_specs=placed, out_specs=P("lat", "lon", None), check_vma=False
    )
```

```python
import math

import jax
import jax.numpy as jnp
from jax import lax
from jax.experimental import pallas as pl
from jax.experimental.pallas import tpu as pltpu
from jax.sharding import PartitionSpec as P

HEADS = 4
BLOCKS = 2
EDGE = 3
CORES = 2
RING = 4
BF = jnp.bfloat16
F32 = jnp.float32
MESH = pl.DeviceIdType.MESH


def conv(src, start, count, spread, weights):
    wide, width = src.shape[1], src.shape[2]
    cells = count * wide
    taps = [src[pl.ds(start + i * spread, count)].reshape(cells, width) for i in range(3)]
    lhs = jnp.concatenate(taps, axis=1)
    parts = [
        jnp.dot(lhs, weights[:, j].reshape(3 * width, width), preferred_element_type=F32)
        for j in range(3)
    ]
    return pltpu.roll(parts[0], spread, 0) + parts[1] + pltpu.roll(parts[2], cells - spread, 0)


def shifted(cells, start, by):
    tile = cells[:, start // 16 * 16 : start // 16 * 16 + 16, :].astype(F32)
    return pltpu.roll(tile[:, start % 16 : start % 16 + 8], by, 1)


def with_edges(ref, index, from_left, from_right):
    count, _, width = from_left.shape
    wide = ref.shape[-2]
    place = lax.broadcasted_iota(jnp.int32, (count, 16, width), 1)
    nothing = jnp.zeros(from_left.shape, F32)
    low = ref[index, 0:16, :].astype(F32)
    high = ref[index, wide - 16 : wide, :].astype(F32)
    ref[index, 0:16, :] = jnp.where(
        place < EDGE, jnp.concatenate([from_left, nothing], axis=1), low
    ).astype(BF)
    ref[index, wide - 16 : wide, :] = jnp.where(
        place >= 16 - EDGE, jnp.concatenate([nothing, from_right], axis=1), high
    ).astype(BF)


def kernel(
    fields_hbm, mask_hbm, w1_hbm, w2_hbm, gain_hbm, wqkv_hbm, wo_hbm, out,
    fields, mask, gain, w1, w2, wqkv, wo, xs, xb, hb, mp, epack, erecv, nself, nbuf, qm, qb, kb, vx, att,
    isem, wsem, e_send, e_recv, l_send, l_recv, m_sem, f_send, f_recv, s_send, s_recv, h_send, x_recv,
):
    cols, rows, width = fields.shape
    wide = cols + 2 * EDGE
    head_dim = width // HEADS
    lats, lons = lax.axis_size("lat"), lax.axis_size("lon")
    chips = lons // CORES
    groups = chips // 2
    half = chips * wide
    lat, lon = lax.axis_index("lat"), lax.axis_index("lon")
    chip, core = lon // CORES, lon % CORES
    z, y_hi = lat // 2, lat % 2
    x_at, y_at = lon // 4, y_hi * 2 + (lon // 2) % 2
    up, down = (lat + lats - 1) % lats, (lat + 1) % lats
    left, right = (lon + lons - 1) % lons, (lon + 1) % lons
    sibling = chip * CORES + 1 - core
    band_1, sector_1 = z * 2 + core, x_at * 4 + (y_at + x_at) % RING

    def place_1(band, sector):
        x = sector // 4
        y = (sector + 3 * x) % RING
        return band // 2 * 2 + y // 2, x * 4 + y % 2 * 2 + band % 2

    def placed(blk, band, sector):
        there = place_1(band, sector)
        return band + blk * (there[0] - band), sector + blk * (there[1] - sector)

    def elsewhere(to):
        return (to[0] != lat) | (to[1] != lon)

    def remote(src, dst, send, recv, to):
        return pltpu.make_async_remote_copy(
            src_ref=src, dst_ref=dst, send_sem=send, recv_sem=recv, device_id=to, device_id_type=MESH
        )

    def each(count, body):
        lax.fori_loop(0, count, lambda k, carry: (body(k), carry)[1], 0)

    def across(k):
        return (x_at + 2 - k + k // 2 * (2 * k - 1) + RING) % RING

    barrier = pltpu.get_barrier_semaphore()

    def greet(to):
        @pl.when(elsewhere(to))
        def _():
            pl.semaphore_signal(barrier, inc=1, device_id=to, device_id_type=MESH)

    up_1 = place_1((band_1 + lats - 1) % lats, sector_1)
    down_1 = place_1((band_1 + 1) % lats, sector_1)

    inputs = [
        pltpu.make_async_copy(mask_hbm, mask, isem.at[0]),
        pltpu.make_async_copy(fields_hbm, fields, isem.at[1]),
        pltpu.make_async_copy(gain_hbm, gain, isem.at[2]),
    ]

    def weight_copies(blk):
        return [
            pltpu.make_async_copy(w1_hbm.at[blk], w1.at[blk], wsem.at[0, blk]),
            pltpu.make_async_copy(w2_hbm.at[blk], w2.at[blk], wsem.at[1, blk]),
            pltpu.make_async_copy(wqkv_hbm.at[blk], wqkv.at[blk], wsem.at[2, blk]),
            pltpu.make_async_copy(wo_hbm.at[blk], wo.at[blk], wsem.at[3, blk]),
        ]

    for copy in inputs:
        copy.start()
    for blk in range(BLOCKS):
        for copy in weight_copies(blk):
            copy.start()

    for to in ((up, lon), (down, lon), (lat, left), (lat, right), (lat, sibling)):
        greet(to)
    each(chips, lambda i: greet((lat, i * CORES + core)))

    for copy in inputs:
        copy.wait()
    xs[0:EDGE] = jnp.zeros((EDGE, rows, width), F32)
    xs[EDGE + cols :] = jnp.zeros((EDGE, rows, width), F32)
    xs[EDGE : EDGE + cols] = fields[...].astype(F32)
    own = pl.ds(EDGE, rows)
    for a in range(rows):
        on = mask[a].astype(F32)
        mp[EDGE + y_hi * rows + a] = jnp.full(mp.shape[1:], on, F32)
        xb[0, EDGE + a] = (xs[:, a, :] * on).astype(BF)
    mp[0:EDGE] = jnp.full((EDGE,) + mp.shape[1:], jnp.where(z > 0, 1.0, 0.0), F32)
    mp[EDGE + 2 * rows :] = jnp.full((EDGE,) + mp.shape[1:], jnp.where(z < lats // 2 - 1, 1.0, 0.0), F32)
    epack[0] = shifted(xb[0, own], 0, 2).reshape(rows * 8, width).astype(BF)
    epack[1] = shifted(xb[0, own], wide - 8, 6).reshape(rows * 8, width).astype(BF)

    pl.semaphore_wait(barrier, 5 + chips - 1)

    def mask_copy():
        both = mp.at[pl.ds(EDGE + y_hi * rows, rows)]
        return remote(both, both, m_sem.at[0], m_sem.at[1], (lat + 1 - 2 * y_hi, lon))

    def edge_copies():
        return [
            remote(epack.at[0], erecv.at[1], e_send.at[0], e_recv.at[1], (lat, left)),
            remote(epack.at[1], erecv.at[0], e_send.at[1], e_recv.at[0], (lat, right)),
        ]

    def row_copies(n):
        blk, to_up, to_down = (1, up_1, down_1) if n == 3 else (0, (up, lon), (down, lon))
        columns = (pl.ds(16, wide - 32), pl.ds(0, 16), pl.ds(wide - 16, 16), pl.ds(0, wide))[n]
        top, bottom = xb.at[blk, pl.ds(EDGE, EDGE), columns], xb.at[blk, pl.ds(rows, EDGE), columns]
        above, below = xb.at[blk, pl.ds(0, EDGE), columns], xb.at[blk, pl.ds(EDGE + rows, EDGE), columns]
        return [
            remote(top, below, l_send.at[n, 0], l_recv.at[n, 1], to_up),
            remote(bottom, above, l_send.at[n, 1], l_recv.at[n, 0], to_down),
        ]

    for copy in edge_copies() + row_copies(0):
        copy.start()
    mask_copy().start()

    for copy in edge_copies():
        copy.wait_recv()
    with_edges(
        xb.at[0], own,
        erecv[0].astype(F32).reshape(rows, 8, width), erecv[1].astype(F32).reshape(rows, 8, width),
    )
    for copy in row_copies(1) + row_copies(2):
        copy.start()

    def row_mask(first, count):
        on = mp[pl.ds(first, count)][:, :1, :]
        return jnp.concatenate([on, on], axis=2)

    def norm(cells, blk):
        mean_of = jnp.full((width, width), 1.0 / width, BF)
        off = cells.astype(F32) - jnp.dot(cells, mean_of, preferred_element_type=F32)
        var = jnp.dot((off * off).astype(BF), mean_of, preferred_element_type=F32)
        return (off * lax.rsqrt(var + 1e-05) * gain[pl.ds(blk, 1)]).astype(BF)

    column = lax.broadcasted_iota(jnp.int32, (1, wide, 1), 1)
    inside = (column >= EDGE) & (column < EDGE + cols)

    def state_copy(blk, i, to_blk, r, to):
        return remote(
            att.at[blk, i], xb.at[to_blk, EDGE + r], h_send.at[blk, i], x_recv.at[to_blk, r], to
        )

    def block(blk):
        x = xb.at[blk]
        w1_copy, w2_copy, wqkv_copy, wo_copy = weight_copies(blk)
        band = lat + blk * (band_1 - lat)
        sector = lon + blk * (sector_1 - lon)
        parity = sector % 2
        first_row = band % 2 * rows

        def arrived(r):
            @pl.when(elsewhere((band_1, r * CORES + sector_1 % 2)))
            def _():
                state_copy(0, 0, 1, r, (lat, sibling)).wait_recv()

        w1_copy.wait()

        @pl.when(blk == 1)
        def _():
            to_up, to_down = row_copies(3)
            each(EDGE, arrived)
            to_up.start()
            each(EDGE, lambda r: arrived(rows - EDGE + r))
            to_down.start()
            each(rows - 2 * EDGE, lambda r: arrived(EDGE + r))

        def first(start):
            got = conv(x, start, EDGE, 1, w1.at[blk])
            got = jax.nn.gelu(got).reshape(EDGE, wide, width) * row_mask(first_row + start + 1, EDGE)
            hb[pl.ds(start, EDGE)] = got.astype(BF)

        each(2, lambda k: first(EDGE * (1 + k)))

        def outer(side):
            def ready(n):
                @pl.when(side == 0)
                def _():
                    row_copies(n)[1].wait_recv()

                @pl.when(side == 1)
                def _():
                    row_copies(n)[0].wait_recv()

            @pl.when(blk == 0)
            def _():
                for n in range(3):
                    ready(n)

            @pl.when(blk == 1)
            def _():
                ready(3)

            @pl.when((side == 0) & (band == 0))
            def _():
                x[0:EDGE] = jnp.zeros((EDGE, wide, width), BF)

            @pl.when((side == 1) & (band == lats - 1))
            def _():
                x[EDGE + rows :] = jnp.zeros((EDGE, wide, width), BF)

            first(3 * EDGE * side)

        w2_copy.wait()

        def row_copy(r):
            return remote(
                nself.at[blk, r], nbuf.at[blk, parity, sector // 2], f_send.at[blk, r],
                f_recv.at[blk, sector // 2], (band, r * CORES + parity),
            )

        @pl.when(blk == 0)
        def _():
            mask_copy().wait_recv()

        def second(k):
            side = (1 - core + k // 2) % 2
            a = side * 4 + (x_at + 1 + side + x_at // 2 + k) % 2 * 2

            @pl.when(k % 2 == 0)
            def _():
                outer(side)

            got = jax.nn.gelu(conv(hb, a, 2, 2, w2.at[blk])).reshape(2, wide, width)
            got = (x[pl.ds(a + EDGE, 2)].astype(F32) + got) * row_mask(first_row + a + EDGE, 2)
            nself[blk, pl.ds(a, 2)] = got.astype(BF)
            for i in range(2):
                r = a + i
                far = elsewhere((band, r * CORES + parity))

                @pl.when(far)
                def _():
                    row_copy(r).start()

                @pl.when(jnp.logical_not(far))
                def _():
                    nbuf[blk, parity, sector // 2] = nself[blk, r]

        each(groups, second)

        def half_copy(i):
            slot = nbuf.at[blk, core, i]
            return remote(slot, slot, s_send.at[blk, i], s_recv.at[blk, i], (lat, sibling))

        def pass_on(k):
            i = across(k // 2) * 2 + k % 2

            @pl.when(elsewhere(placed(blk, lat, i * CORES + core)))
            def _():
                remote(
                    nself.at[blk, i], nbuf.at[blk, core, i], f_send.at[blk, i], f_recv.at[blk, i],
                    (lat, sibling),
                ).wait_recv()

            half_copy(i).start()

        each(chips, pass_on)

        wqkv_copy.wait()
        first_head = lax.broadcasted_iota(jnp.int32, (1, 1, 2 * head_dim), 2) < head_dim
        ones = jnp.where(inside, 1.0, 0.0)

        scale = math.log2(math.e) / math.sqrt(head_dim)

        def set_query(cells):
            query = jnp.dot(cells, wqkv[blk, :, :width], preferred_element_type=F32)
            qb[...] = (query * scale).astype(BF).reshape(chips, wide, width)

        def keys_values(t):
            side = (core + t) % CORES

            @pl.when(t == 1)
            def _():
                each(chips, lambda i: half_copy(i).wait_recv())

            cells = norm(nbuf[blk, side].reshape(half, width), blk)

            @pl.when((t == 0) & (blk == BLOCKS - 1))
            def _():
                set_query(cells)

            cells = jnp.where(inside, cells.reshape(chips, wide, width), jnp.zeros((), BF))
            cells = cells.reshape(half, width)
            both = jnp.dot(cells, wqkv[blk, :, width:], preferred_element_type=F32)
            kb[side] = both[:, :width].astype(BF).reshape(chips, wide, width)
            values = both[:, width:].reshape(chips, wide, width)
            for h in range(HEADS):
                pair = values[:, :, h // 2 * 2 * head_dim :][:, :, : 2 * head_dim]
                keep = first_head if h % 2 == 0 else ~first_head
                vx[h, side] = jnp.where(keep, pair, ones).astype(BF).reshape(vx.shape[2:])

        qm[...] = nbuf[blk, core]
        each(CORES, keys_values)

        def join(i):
            before, after = (i + chips - 1 + core) % chips, (i + core) % chips
            from_left = shifted(nbuf[blk, 1 - core, pl.ds(before, 1)], wide - 8, 6)
            from_right = shifted(nbuf[blk, 1 - core, pl.ds(after, 1)], 0, 2)
            with_edges(qm, pl.ds(i, 1), from_left, from_right)

        @pl.when(blk < BLOCKS - 1)
        def _():
            each(chips, join)
            set_query(norm(qm[...].reshape(half, width), blk))

        wo_copy.wait()

        def home_copy(i):
            to = placed(1 - blk, lat, i * CORES + core)
            return to, state_copy(blk, i, blk + 1, chip, to)

        def attend(k):
            a = across(k) * 2
            query = qb[pl.ds(a, 2)].reshape(2 * wide, width)
            low_lane = lax.broadcasted_iota(jnp.int32, (1, 2 * head_dim), 1) < head_dim
            zero = jnp.zeros((), BF)
            attended = []
            for p in range(HEADS // 2):
                span = slice(p * 2 * head_dim, (p + 1) * 2 * head_dim)
                both = query[:, span]
                lhs = jnp.concatenate(
                    [jnp.where(low_lane, both, zero), jnp.where(low_lane, zero, both)], axis=0
                )
                keys = kb[:, :, :, span].reshape(CORES * half, 2 * head_dim)
                scores = lax.dot_general(
                    lhs, keys, (((1,), (1,)), ((), ())), preferred_element_type=F32
                )
                expo = jnp.exp2(scores).astype(BF)
                got = []
                for e in range(2):
                    values = vx[2 * p + e].reshape(CORES * half, 2 * head_dim)
                    part = jnp.dot(
                        expo[e * 2 * wide : (e + 1) * 2 * wide], values, preferred_element_type=F32
                    )
                    got.append(part / pltpu.roll(part, head_dim, 1))
                attended.append(jnp.where(low_lane, got[0], got[1]).astype(BF))
            update = jnp.dot(
                jnp.concatenate(attended, axis=1), wo[blk], preferred_element_type=F32
            )
            state = qm[pl.ds(a, 2)].astype(F32) + update.reshape(2, wide, width)
            state = state * row_mask(EDGE + y_hi * rows + chip, 1)
            att[blk, pl.ds(a, 2)] = state.astype(BF)
            for n in range(2):
                i = a + n
                to, copy = home_copy(i)
                far = elsewhere(to)

                @pl.when(far)
                def _():
                    copy.start()

                @pl.when(jnp.logical_not(far))
                def _():
                    xb[blk + 1, EDGE + chip] = att[blk, i]

        each(groups, attend)

    each(BLOCKS, block)

    def sent(blk):
        band = lat + blk * (band_1 - lat)
        parity = (lon + blk * (sector_1 - lon)) % 2

        def one(i):
            @pl.when(elsewhere((band, i * CORES + parity)))
            def _():
                remote(
                    nself.at[blk, i], nbuf.at[blk, core, i], f_send.at[blk, i], f_recv.at[blk, i], (lat, sibling)
                ).wait_send()

            slot = nbuf.at[blk, core, i]
            remote(slot, slot, s_send.at[blk, i], s_recv.at[blk, i], (lat, sibling)).wait_send()

            @pl.when(elsewhere(placed(1 - blk, lat, i * CORES + core)))
            def _():
                state_copy(blk, i, blk + 1, chip, (lat, sibling)).wait_send()

        each(chips, one)

    each(BLOCKS, sent)

    for copy in edge_copies() + sum((row_copies(n) for n in range(4)), []) + [mask_copy()]:
        copy.wait_send()

    def come_home(r):
        @pl.when(r != chip)
        def _():
            state_copy(0, 0, BLOCKS, r, (lat, sibling)).wait_recv()

    each(rows, come_home)
    out[...] = xb[BLOCKS, own]


def body(fields, lat_mask, conv_first, conv_second, norm_gain, qkv_weight, out_weight):
    rows, cols, width = fields.shape
    wide = cols + 2 * EDGE
    chips = lax.axis_size("lon") // CORES
    head_dim = width // HEADS
    vmem = pl.BlockSpec(memory_space=pltpu.VMEM)
    hbm = pl.BlockSpec(memory_space=pltpu.HBM)
    dma = pltpu.SemaphoreType.DMA
    wide_out = pl.pallas_call(
        kernel,
        out_shape=pltpu.VMEM((rows, wide, width), BF),
        in_specs=[hbm] * 7,
        out_specs=vmem,
        scratch_shapes=[
            pltpu.VMEM((cols, rows, width), BF),
            pltpu.SMEM(lat_mask.shape, jnp.int32),
            pltpu.VMEM(norm_gain.shape, F32),
            pltpu.VMEM(conv_first.shape, BF),
            pltpu.VMEM(conv_second.shape, BF),
            pltpu.VMEM(qkv_weight.shape, BF),
            pltpu.VMEM(out_weight.shape, BF),
            pltpu.VMEM((wide, rows, width), F32),
            pltpu.VMEM((BLOCKS + 1, rows + 2 * EDGE, wide, width), BF),
            pltpu.VMEM((rows + 4, wide, width), BF),
            pltpu.VMEM((2 * rows + 2 * EDGE, 8, width // 2), F32),
            pltpu.VMEM((2, rows * 8, width), BF),
            pltpu.VMEM((2, rows * 8, width), BF),
            pltpu.VMEM((BLOCKS, rows, wide, width), BF),
            pltpu.VMEM((BLOCKS, CORES, chips, wide, width), BF),
            pltpu.VMEM((chips, wide, width), BF),
            pltpu.VMEM((chips, wide, width), BF),
            pltpu.VMEM((CORES, chips, wide, width), BF),
            pltpu.VMEM((HEADS, CORES, chips, wide, 2 * head_dim), BF),
            pltpu.VMEM((BLOCKS, chips, wide, width), BF),
            dma((3,)),
            dma((4, BLOCKS)),
            dma((2,)),
            dma((2,)),
            dma((4, 2)),
            dma((4, 2)),
            dma((2,)),
            dma((BLOCKS, rows)),
            dma((BLOCKS, chips)),
            dma((BLOCKS, chips)),
            dma((BLOCKS, chips)),
            dma((BLOCKS, chips)),
            dma((BLOCKS + 1, rows)),
        ],
        compiler_params=pltpu.CompilerParams(
            collective_id=0, has_side_effects=True, vmem_limit_bytes=60 * 1024 * 1024
        ),
    )(jnp.transpose(fields, (1, 0, 2)), lat_mask, conv_first, conv_second, norm_gain, qkv_weight, out_weight)
    return wide_out[:, EDGE : EDGE + cols]


def solution(mesh):
    placed = (P("lat", "lon", None), P("lat"), P(), P(), P(), P(), P())
    return jax.shard_map(
        body, mesh=mesh, in_specs=placed, out_specs=P("lat", "lon", None), check_vma=False
    )
```

```python
import math

import jax
import jax.numpy as jnp
from jax import lax
from jax.experimental import pallas as pl
from jax.experimental.pallas import tpu as pltpu
from jax.sharding import PartitionSpec as P

HEADS = 4
BLOCKS = 2
EDGE = 3
CORES = 2
RING = 4
BF = jnp.bfloat16
F32 = jnp.float32
MESH = pl.DeviceIdType.MESH


def conv(src, start, count, spread, weights):
    wide, width = src.shape[1], src.shape[2]
    cells = count * wide
    taps = [src[pl.ds(start + i * spread, count)].reshape(cells, width) for i in range(3)]
    lhs = jnp.concatenate(taps, axis=1)
    parts = [
        jnp.dot(lhs, weights[:, j].reshape(3 * width, width), preferred_element_type=F32)
        for j in range(3)
    ]
    return pltpu.roll(parts[0], spread, 0) + parts[1] + pltpu.roll(parts[2], cells - spread, 0)


def shifted(cells, start, by):
    tile = cells[:, start // 16 * 16 : start // 16 * 16 + 16, :].astype(F32)
    return pltpu.roll(tile[:, start % 16 : start % 16 + 8], by, 1)


def with_edges(ref, index, from_left, from_right):
    count, _, width = from_left.shape
    wide = ref.shape[-2]
    place = lax.broadcasted_iota(jnp.int32, (count, 16, width), 1)
    nothing = jnp.zeros(from_left.shape, F32)
    low = ref[index, 0:16, :].astype(F32)
    high = ref[index, wide - 16 : wide, :].astype(F32)
    ref[index, 0:16, :] = jnp.where(
        place < EDGE, jnp.concatenate([from_left, nothing], axis=1), low
    ).astype(BF)
    ref[index, wide - 16 : wide, :] = jnp.where(
        place >= 16 - EDGE, jnp.concatenate([nothing, from_right], axis=1), high
    ).astype(BF)


def kernel(
    fields_hbm, mask_hbm, w1_hbm, w2_hbm, gain_hbm, wqkv_hbm, wo_hbm, out,
    fields, mask, gain, w1, w2, wqkv, wo, xs, xb, hb, mp, epack, erecv, nself, nbuf, qm, qb, kb, vx, att,
    isem, wsem, e_send, e_recv, l_send, l_recv, m_sem, f_send, f_recv, s_send, s_recv, h_send, x_recv,
):
    cols, rows, width = fields.shape
    wide = cols + 2 * EDGE
    head_dim = width // HEADS
    lats, lons = lax.axis_size("lat"), lax.axis_size("lon")
    chips = lons // CORES
    groups = chips // 2
    half = chips * wide
    lat, lon = lax.axis_index("lat"), lax.axis_index("lon")
    chip, core = lon // CORES, lon % CORES
    z, y_hi = lat // 2, lat % 2
    x_at, y_at = lon // 4, y_hi * 2 + (lon // 2) % 2
    up, down = (lat + lats - 1) % lats, (lat + 1) % lats
    left, right = (lon + lons - 1) % lons, (lon + 1) % lons
    sibling = chip * CORES + 1 - core
    band_1, sector_1 = z * 2 + core, x_at * 4 + (y_at + x_at) % RING

    def place_1(band, sector):
        x = sector // 4
        y = (sector + 3 * x) % RING
        return band // 2 * 2 + y // 2, x * 4 + y % 2 * 2 + band % 2

    def placed(blk, band, sector):
        there = place_1(band, sector)
        return band + blk * (there[0] - band), sector + blk * (there[1] - sector)

    def elsewhere(to):
        return (to[0] != lat) | (to[1] != lon)

    def remote(src, dst, send, recv, to):
        return pltpu.make_async_remote_copy(
            src_ref=src, dst_ref=dst, send_sem=send, recv_sem=recv, device_id=to, device_id_type=MESH
        )

    def each(count, body):
        lax.fori_loop(0, count, lambda k, carry: (body(k), carry)[1], 0)

    def across(k):
        return (x_at + 2 - k + k // 2 * (2 * k - 1) + RING) % RING

    barrier = pltpu.get_barrier_semaphore()

    def greet(to):
        @pl.when(elsewhere(to))
        def _():
            pl.semaphore_signal(barrier, inc=1, device_id=to, device_id_type=MESH)

    up_1 = place_1((band_1 + lats - 1) % lats, sector_1)
    down_1 = place_1((band_1 + 1) % lats, sector_1)

    for to in ((up, lon), (down, lon), (lat, left), (lat, right), (lat, sibling)):
        greet(to)
    each(chips, lambda i: greet((lat, i * CORES + core)))

    inputs = [
        pltpu.make_async_copy(mask_hbm, mask, isem.at[0]),
        pltpu.make_async_copy(fields_hbm, fields, isem.at[1]),
        pltpu.make_async_copy(gain_hbm, gain, isem.at[2]),
    ]

    def weight_copies(blk):
        return [
            pltpu.make_async_copy(w1_hbm.at[blk], w1.at[blk], wsem.at[0, blk]),
            pltpu.make_async_copy(w2_hbm.at[blk], w2.at[blk], wsem.at[1, blk]),
            pltpu.make_async_copy(wqkv_hbm.at[blk], wqkv.at[blk], wsem.at[2, blk]),
            pltpu.make_async_copy(wo_hbm.at[blk], wo.at[blk], wsem.at[3, blk]),
        ]

    for copy in inputs:
        copy.start()
    for blk in range(BLOCKS):
        for copy in weight_copies(blk):
            copy.start()

    for copy in inputs:
        copy.wait()
    xs[0:EDGE] = jnp.zeros((EDGE, rows, width), F32)
    xs[EDGE + cols :] = jnp.zeros((EDGE, rows, width), F32)
    xs[EDGE : EDGE + cols] = fields[...].astype(F32)
    own = pl.ds(EDGE, rows)
    for a in range(rows):
        on = mask[a].astype(F32)
        mp[EDGE + y_hi * rows + a] = jnp.full(mp.shape[1:], on, F32)
        xb[0, EDGE + a] = (xs[:, a, :] * on).astype(BF)
    mp[0:EDGE] = jnp.full((EDGE,) + mp.shape[1:], jnp.where(z > 0, 1.0, 0.0), F32)
    mp[EDGE + 2 * rows :] = jnp.full((EDGE,) + mp.shape[1:], jnp.where(z < lats // 2 - 1, 1.0, 0.0), F32)
    epack[0] = shifted(xb[0, own], 0, 2).reshape(rows * 8, width).astype(BF)
    epack[1] = shifted(xb[0, own], wide - 8, 6).reshape(rows * 8, width).astype(BF)

    pl.semaphore_wait(barrier, 5 + chips - 1)

    def mask_copy():
        both = mp.at[pl.ds(EDGE + y_hi * rows, rows)]
        return remote(both, both, m_sem.at[0], m_sem.at[1], (lat + 1 - 2 * y_hi, lon))

    def edge_copies():
        return [
            remote(epack.at[0], erecv.at[1], e_send.at[0], e_recv.at[1], (lat, left)),
            remote(epack.at[1], erecv.at[0], e_send.at[1], e_recv.at[0], (lat, right)),
        ]

    def row_copies(n):
        blk, to_up, to_down = (1, up_1, down_1) if n == 3 else (0, (up, lon), (down, lon))
        columns = (pl.ds(16, wide - 32), pl.ds(0, 16), pl.ds(wide - 16, 16), pl.ds(0, wide))[n]
        top, bottom = xb.at[blk, pl.ds(EDGE, EDGE), columns], xb.at[blk, pl.ds(rows, EDGE), columns]
        above, below = xb.at[blk, pl.ds(0, EDGE), columns], xb.at[blk, pl.ds(EDGE + rows, EDGE), columns]
        return [
            remote(top, below, l_send.at[n, 0], l_recv.at[n, 1], to_up),
            remote(bottom, above, l_send.at[n, 1], l_recv.at[n, 0], to_down),
        ]

    for copy in edge_copies() + row_copies(0):
        copy.start()
    mask_copy().start()

    for copy in edge_copies():
        copy.wait_recv()
    with_edges(
        xb.at[0], own,
        erecv[0].astype(F32).reshape(rows, 8, width), erecv[1].astype(F32).reshape(rows, 8, width),
    )
    for copy in row_copies(1) + row_copies(2):
        copy.start()

    def row_mask(first, count):
        on = mp[pl.ds(first, count)][:, :1, :]
        return jnp.concatenate([on, on], axis=2)

    def norm(cells, blk):
        mean_of = jnp.full((width, width), 1.0 / width, BF)
        off = cells.astype(F32) - jnp.dot(cells, mean_of, preferred_element_type=F32)
        var = jnp.dot((off * off).astype(BF), mean_of, preferred_element_type=F32)
        return (off * lax.rsqrt(var + 1e-05) * gain[pl.ds(blk, 1)]).astype(BF)

    column = lax.broadcasted_iota(jnp.int32, (1, wide, 1), 1)
    inside = (column >= EDGE) & (column < EDGE + cols)

    def state_copy(blk, i, to_blk, r, to):
        return remote(
            att.at[blk, i], xb.at[to_blk, EDGE + r], h_send.at[blk, i], x_recv.at[to_blk, r], to
        )

    def block(blk):
        x = xb.at[blk]
        w1_copy, w2_copy, wqkv_copy, wo_copy = weight_copies(blk)
        band = lat + blk * (band_1 - lat)
        sector = lon + blk * (sector_1 - lon)
        parity = sector % 2
        first_row = band % 2 * rows

        def arrived(r):
            @pl.when(elsewhere((band_1, r * CORES + sector_1 % 2)))
            def _():
                state_copy(0, 0, 1, r, (lat, sibling)).wait_recv()

        w1_copy.wait()

        @pl.when(blk == 1)
        def _():
            to_up, to_down = row_copies(3)
            each(EDGE, arrived)
            to_up.start()
            each(EDGE, lambda r: arrived(rows - EDGE + r))
            to_down.start()
            each(rows - 2 * EDGE, lambda r: arrived(EDGE + r))

        def first(start, count):
            got = conv(x, start, count, 1, w1.at[blk])
            got = jax.nn.gelu(got).reshape(count, wide, width) * row_mask(first_row + start + 1, count)
            hb[pl.ds(start, count)] = got.astype(BF)

        first(EDGE, rows - 2)

        def outer(side):
            def ready(n):
                @pl.when(side == 0)
                def _():
                    row_copies(n)[1].wait_recv()

                @pl.when(side == 1)
                def _():
                    row_copies(n)[0].wait_recv()

            @pl.when(blk == 0)
            def _():
                for n in range(3):
                    ready(n)

            @pl.when(blk == 1)
            def _():
                ready(3)

            @pl.when((side == 0) & (band == 0))
            def _():
                x[0:EDGE] = jnp.zeros((EDGE, wide, width), BF)

            @pl.when((side == 1) & (band == lats - 1))
            def _():
                x[EDGE + rows :] = jnp.zeros((EDGE, wide, width), BF)

            first(3 * EDGE * side, EDGE)

        w2_copy.wait()

        def row_copy(r):
            return remote(
                nself.at[blk, r], nbuf.at[blk, parity, sector // 2], f_send.at[blk, r],
                f_recv.at[blk, sector // 2], (band, r * CORES + parity),
            )

        @pl.when(blk == 0)
        def _():
            mask_copy().wait_recv()

        def second(k):
            side = (1 - core + k // 2) % 2
            a = side * 4 + (x_at + 1 + side + x_at // 2 + k) % 2 * 2

            @pl.when(k % 2 == 0)
            def _():
                outer(side)

            got = jax.nn.gelu(conv(hb, a, 2, 2, w2.at[blk])).reshape(2, wide, width)
            got = (x[pl.ds(a + EDGE, 2)].astype(F32) + got) * row_mask(first_row + a + EDGE, 2)
            nself[blk, pl.ds(a, 2)] = got.astype(BF)
            for i in range(2):
                r = a + i
                far = elsewhere((band, r * CORES + parity))

                @pl.when(far)
                def _():
                    row_copy(r).start()

                @pl.when(jnp.logical_not(far))
                def _():
                    nbuf[blk, parity, sector // 2] = nself[blk, r]

        each(groups, second)

        def half_copy(i):
            slot = nbuf.at[blk, core, i]
            return remote(slot, slot, s_send.at[blk, i], s_recv.at[blk, i], (lat, sibling))

        def pass_on(k):
            i = across(k // 2) * 2 + k % 2

            @pl.when(elsewhere(placed(blk, lat, i * CORES + core)))
            def _():
                remote(
                    nself.at[blk, i], nbuf.at[blk, core, i], f_send.at[blk, i], f_recv.at[blk, i],
                    (lat, sibling),
                ).wait_recv()

            half_copy(i).start()

        each(chips, pass_on)

        wqkv_copy.wait()
        first_head = lax.broadcasted_iota(jnp.int32, (1, 1, 2 * head_dim), 2) < head_dim
        ones = jnp.where(inside, 1.0, 0.0)

        scale = math.log2(math.e) / math.sqrt(head_dim)

        def query(cells):
            found = jnp.dot(cells, wqkv[blk, :, :width], preferred_element_type=F32)
            return (found * scale).astype(BF).reshape(chips, -1, width)

        def keys_values(t):
            side = (core + t) % CORES

            @pl.when(t == 1)
            def _():
                each(chips, lambda i: half_copy(i).wait_recv())

            cells = norm(nbuf[blk, side].reshape(half, width), blk)

            @pl.when(t == 0)
            def _():
                qb[...] = query(cells)

            cells = jnp.where(inside, cells.reshape(chips, wide, width), jnp.zeros((), BF))
            cells = cells.reshape(half, width)
            both = jnp.dot(cells, wqkv[blk, :, width:], preferred_element_type=F32)
            kb[side] = both[:, :width].astype(BF).reshape(chips, wide, width)
            values = both[:, width:].reshape(chips, wide, width)
            for h in range(HEADS):
                pair = values[:, :, h // 2 * 2 * head_dim :][:, :, : 2 * head_dim]
                keep = first_head if h % 2 == 0 else ~first_head
                vx[h, side] = jnp.where(keep, pair, ones).astype(BF).reshape(vx.shape[2:])

        qm[...] = nbuf[blk, core]
        each(CORES, keys_values)

        def join(i):
            before, after = (i + chips - 1 + core) % chips, (i + core) % chips
            from_left = shifted(nbuf[blk, 1 - core, pl.ds(before, 1)], wide - 8, 6)
            from_right = shifted(nbuf[blk, 1 - core, pl.ds(after, 1)], 0, 2)
            with_edges(qm, pl.ds(i, 1), from_left, from_right)

        @pl.when(blk < BLOCKS - 1)
        def _():
            for i in range(chips):
                join(i)
            for ends in (slice(0, 16), slice(wide - 16, wide)):
                qb[:, ends] = query(norm(qm[:, ends].reshape(chips * 16, width), blk))

        wo_copy.wait()

        def home_copy(i):
            to = placed(1 - blk, lat, i * CORES + core)
            return to, state_copy(blk, i, blk + 1, chip, to)

        def attend(k):
            a = across(k) * 2
            query = qb[pl.ds(a, 2)].reshape(2 * wide, width)
            low_lane = lax.broadcasted_iota(jnp.int32, (1, 2 * head_dim), 1) < head_dim
            zero = jnp.zeros((), BF)
            attended = []
            for p in range(HEADS // 2):
                span = slice(p * 2 * head_dim, (p + 1) * 2 * head_dim)
                both = query[:, span]
                lhs = jnp.concatenate(
                    [jnp.where(low_lane, both, zero), jnp.where(low_lane, zero, both)], axis=0
                )
                keys = kb[:, :, :, span].reshape(CORES * half, 2 * head_dim)
                scores = lax.dot_general(
                    lhs, keys, (((1,), (1,)), ((), ())), preferred_element_type=F32
                )
                expo = jnp.exp2(scores).astype(BF)
                got = []
                for e in range(2):
                    values = vx[2 * p + e].reshape(CORES * half, 2 * head_dim)
                    part = jnp.dot(
                        expo[e * 2 * wide : (e + 1) * 2 * wide], values, preferred_element_type=F32
                    )
                    got.append(part / pltpu.roll(part, head_dim, 1))
                attended.append(jnp.where(low_lane, got[0], got[1]).astype(BF))
            update = jnp.dot(
                jnp.concatenate(attended, axis=1), wo[blk], preferred_element_type=F32
            )
            state = qm[pl.ds(a, 2)].astype(F32) + update.reshape(2, wide, width)
            state = state * row_mask(EDGE + y_hi * rows + chip, 1)
            att[blk, pl.ds(a, 2)] = state.astype(BF)
            for n in range(2):
                i = a + n
                to, copy = home_copy(i)
                far = elsewhere(to)

                @pl.when(far)
                def _():
                    copy.start()

                @pl.when(jnp.logical_not(far))
                def _():
                    xb[blk + 1, EDGE + chip] = att[blk, i]

        each(groups, attend)

    each(BLOCKS, block)

    def sent(blk):
        band = lat + blk * (band_1 - lat)
        parity = (lon + blk * (sector_1 - lon)) % 2

        def one(i):
            @pl.when(elsewhere((band, i * CORES + parity)))
            def _():
                remote(
                    nself.at[blk, i], nbuf.at[blk, core, i], f_send.at[blk, i], f_recv.at[blk, i], (lat, sibling)
                ).wait_send()

            slot = nbuf.at[blk, core, i]
            remote(slot, slot, s_send.at[blk, i], s_recv.at[blk, i], (lat, sibling)).wait_send()

            @pl.when(elsewhere(placed(1 - blk, lat, i * CORES + core)))
            def _():
                state_copy(blk, i, blk + 1, chip, (lat, sibling)).wait_send()

        each(chips, one)

    each(BLOCKS, sent)

    for copy in edge_copies() + sum((row_copies(n) for n in range(4)), []) + [mask_copy()]:
        copy.wait_send()

    def come_home(r):
        @pl.when(r != chip)
        def _():
            state_copy(0, 0, BLOCKS, r, (lat, sibling)).wait_recv()

    each(rows, come_home)
    out[...] = xb[BLOCKS, own]


def body(fields, lat_mask, conv_first, conv_second, norm_gain, qkv_weight, out_weight):
    rows, cols, width = fields.shape
    wide = cols + 2 * EDGE
    chips = lax.axis_size("lon") // CORES
    head_dim = width // HEADS
    vmem = pl.BlockSpec(memory_space=pltpu.VMEM)
    hbm = pl.BlockSpec(memory_space=pltpu.HBM)
    dma = pltpu.SemaphoreType.DMA
    wide_out = pl.pallas_call(
        kernel,
        out_shape=pltpu.VMEM((rows, wide, width), BF),
        in_specs=[hbm] * 7,
        out_specs=vmem,
        scratch_shapes=[
            pltpu.VMEM((cols, rows, width), BF),
            pltpu.SMEM(lat_mask.shape, jnp.int32),
            pltpu.VMEM(norm_gain.shape, F32),
            pltpu.VMEM(conv_first.shape, BF),
            pltpu.VMEM(conv_second.shape, BF),
            pltpu.VMEM(qkv_weight.shape, BF),
            pltpu.VMEM(out_weight.shape, BF),
            pltpu.VMEM((wide, rows, width), F32),
            pltpu.VMEM((BLOCKS + 1, rows + 2 * EDGE, wide, width), BF),
            pltpu.VMEM((rows + 4, wide, width), BF),
            pltpu.VMEM((2 * rows + 2 * EDGE, 8, width // 2), F32),
            pltpu.VMEM((2, rows * 8, width), BF),
            pltpu.VMEM((2, rows * 8, width), BF),
            pltpu.VMEM((BLOCKS, rows, wide, width), BF),
            pltpu.VMEM((BLOCKS, CORES, chips, wide, width), BF),
            pltpu.VMEM((chips, wide, width), BF),
            pltpu.VMEM((chips, wide, width), BF),
            pltpu.VMEM((CORES, chips, wide, width), BF),
            pltpu.VMEM((HEADS, CORES, chips, wide, 2 * head_dim), BF),
            pltpu.VMEM((BLOCKS, chips, wide, width), BF),
            dma((3,)),
            dma((4, BLOCKS)),
            dma((2,)),
            dma((2,)),
            dma((4, 2)),
            dma((4, 2)),
            dma((2,)),
            dma((BLOCKS, rows)),
            dma((BLOCKS, chips)),
            dma((BLOCKS, chips)),
            dma((BLOCKS, chips)),
            dma((BLOCKS, chips)),
            dma((BLOCKS + 1, rows)),
        ],
        compiler_params=pltpu.CompilerParams(
            collective_id=0, has_side_effects=True, vmem_limit_bytes=60 * 1024 * 1024
        ),
    )(jnp.transpose(fields, (1, 0, 2)), lat_mask, conv_first, conv_second, norm_gain, qkv_weight, out_weight)
    return wide_out[:, EDGE : EDGE + cols]


def solution(mesh):
    placed = (P("lat", "lon", None), P("lat"), P(), P(), P(), P(), P())
    return jax.shard_map(
        body, mesh=mesh, in_specs=placed, out_specs=P("lat", "lon", None), check_vma=False
    )
```

```python
import math

import jax
import jax.numpy as jnp
from jax import lax
from jax.experimental import pallas as pl
from jax.experimental.pallas import tpu as pltpu
from jax.sharding import PartitionSpec as P

HEADS = 4
BLOCKS = 2
EDGE = 3
CORES = 2
RING = 4
BF = jnp.bfloat16
F32 = jnp.float32
MESH = pl.DeviceIdType.MESH


def conv(src, start, count, spread, weights):
    wide, width = src.shape[1], src.shape[2]
    cells = count * wide
    taps = [src[pl.ds(start + i * spread, count)].reshape(cells, width) for i in range(3)]
    lhs = jnp.concatenate(taps, axis=1)
    parts = [
        jnp.dot(lhs, weights[:, j].reshape(3 * width, width), preferred_element_type=F32)
        for j in range(3)
    ]
    return pltpu.roll(parts[0], spread, 0) + parts[1] + pltpu.roll(parts[2], cells - spread, 0)


def shifted(cells, start, by):
    tile = cells[:, start // 16 * 16 : start // 16 * 16 + 16, :].astype(F32)
    return pltpu.roll(tile[:, start % 16 : start % 16 + 8], by, 1)


def with_edges(ref, index, from_left, from_right):
    count, _, width = from_left.shape
    wide = ref.shape[-2]
    place = lax.broadcasted_iota(jnp.int32, (count, 16, width), 1)
    nothing = jnp.zeros(from_left.shape, F32)
    low = ref[index, 0:16, :].astype(F32)
    high = ref[index, wide - 16 : wide, :].astype(F32)
    ref[index, 0:16, :] = jnp.where(
        place < EDGE, jnp.concatenate([from_left, nothing], axis=1), low
    ).astype(BF)
    ref[index, wide - 16 : wide, :] = jnp.where(
        place >= 16 - EDGE, jnp.concatenate([nothing, from_right], axis=1), high
    ).astype(BF)


def kernel(
    fields_hbm, mask_hbm, w1_hbm, w2_hbm, gain_hbm, wqkv_hbm, wo_hbm, out,
    fields, mask, gain, w1, w2, wqkv, wo, xs, xb, hb, mp, epack, erecv, nself, nbuf, qm, qb, kb, vx, att,
    isem, wsem, e_send, e_recv, l_send, l_recv, m_sem, f_send, f_recv, s_send, s_recv, h_send, x_recv,
):
    cols, rows, width = fields.shape
    wide = cols + 2 * EDGE
    head_dim = width // HEADS
    lats, lons = lax.axis_size("lat"), lax.axis_size("lon")
    chips = lons // CORES
    groups = chips // 2
    half = chips * wide
    lat, lon = lax.axis_index("lat"), lax.axis_index("lon")
    chip, core = lon // CORES, lon % CORES
    z, y_hi = lat // 2, lat % 2
    x_at, y_at = lon // 4, y_hi * 2 + (lon // 2) % 2
    up, down = (lat + lats - 1) % lats, (lat + 1) % lats
    left, right = (lon + lons - 1) % lons, (lon + 1) % lons
    sibling = chip * CORES + 1 - core
    band_1, sector_1 = z * 2 + core, x_at * 4 + (y_at + x_at) % RING

    def place_1(band, sector):
        x = sector // 4
        y = (sector + 3 * x) % RING
        return band // 2 * 2 + y // 2, x * 4 + y % 2 * 2 + band % 2

    def placed(blk, band, sector):
        there = place_1(band, sector)
        return band + blk * (there[0] - band), sector + blk * (there[1] - sector)

    def elsewhere(to):
        return (to[0] != lat) | (to[1] != lon)

    def remote(src, dst, send, recv, to):
        return pltpu.make_async_remote_copy(
            src_ref=src, dst_ref=dst, send_sem=send, recv_sem=recv, device_id=to, device_id_type=MESH
        )

    def each(count, body):
        lax.fori_loop(0, count, lambda k, carry: (body(k), carry)[1], 0)

    def across(k):
        return (x_at + 2 - k + k // 2 * (2 * k - 1) + RING) % RING

    barrier = pltpu.get_barrier_semaphore()

    def greet(to):
        @pl.when(elsewhere(to))
        def _():
            pl.semaphore_signal(barrier, inc=1, device_id=to, device_id_type=MESH)

    up_1 = place_1((band_1 + lats - 1) % lats, sector_1)
    down_1 = place_1((band_1 + 1) % lats, sector_1)

    for to in ((up, lon), (down, lon), (lat, left), (lat, right), (lat, sibling)):
        greet(to)
    each(chips, lambda i: greet((lat, i * CORES + core)))

    inputs = [
        pltpu.make_async_copy(mask_hbm, mask, isem.at[0]),
        pltpu.make_async_copy(fields_hbm, fields, isem.at[1]),
        pltpu.make_async_copy(gain_hbm, gain, isem.at[2]),
    ]

    def weight_copies(blk):
        return [
            pltpu.make_async_copy(w1_hbm.at[blk], w1.at[blk], wsem.at[0, blk]),
            pltpu.make_async_copy(w2_hbm.at[blk], w2.at[blk], wsem.at[1, blk]),
            pltpu.make_async_copy(wqkv_hbm.at[blk], wqkv.at[blk], wsem.at[2, blk]),
            pltpu.make_async_copy(wo_hbm.at[blk], wo.at[blk], wsem.at[3, blk]),
        ]

    for copy in inputs:
        copy.start()
    for blk in range(BLOCKS):
        for copy in weight_copies(blk):
            copy.start()

    for copy in inputs:
        copy.wait()
    xs[0:EDGE] = jnp.zeros((EDGE, rows, width), F32)
    xs[EDGE + cols :] = jnp.zeros((EDGE, rows, width), F32)
    xs[EDGE : EDGE + cols] = fields[...].astype(F32)
    own = pl.ds(EDGE, rows)
    for a in range(rows):
        on = mask[a].astype(F32)
        mp[EDGE + y_hi * rows + a] = jnp.full(mp.shape[1:], on, F32)
        xb[0, EDGE + a] = (xs[:, a, :] * on).astype(BF)
    mp[0:EDGE] = jnp.full((EDGE,) + mp.shape[1:], jnp.where(z > 0, 1.0, 0.0), F32)
    mp[EDGE + 2 * rows :] = jnp.full((EDGE,) + mp.shape[1:], jnp.where(z < lats // 2 - 1, 1.0, 0.0), F32)
    epack[0] = shifted(xb[0, own], 0, 2).reshape(rows * 8, width).astype(BF)
    epack[1] = shifted(xb[0, own], wide - 8, 6).reshape(rows * 8, width).astype(BF)

    pl.semaphore_wait(barrier, 5 + chips - 1)

    def mask_copy():
        both = mp.at[pl.ds(EDGE + y_hi * rows, rows)]
        return remote(both, both, m_sem.at[0], m_sem.at[1], (lat + 1 - 2 * y_hi, lon))

    def edge_copies():
        return [
            remote(epack.at[0], erecv.at[1], e_send.at[0], e_recv.at[1], (lat, left)),
            remote(epack.at[1], erecv.at[0], e_send.at[1], e_recv.at[0], (lat, right)),
        ]

    def row_copies(n):
        blk, to_up, to_down = (1, up_1, down_1) if n == 3 else (0, (up, lon), (down, lon))
        columns = (pl.ds(16, wide - 32), pl.ds(0, 16), pl.ds(wide - 16, 16), pl.ds(0, wide))[n]
        top, bottom = xb.at[blk, pl.ds(EDGE, EDGE), columns], xb.at[blk, pl.ds(rows, EDGE), columns]
        above, below = xb.at[blk, pl.ds(0, EDGE), columns], xb.at[blk, pl.ds(EDGE + rows, EDGE), columns]
        return [
            remote(top, below, l_send.at[n, 0], l_recv.at[n, 1], to_up),
            remote(bottom, above, l_send.at[n, 1], l_recv.at[n, 0], to_down),
        ]

    for copy in edge_copies() + row_copies(0):
        copy.start()
    mask_copy().start()

    for copy in edge_copies():
        copy.wait_recv()
    with_edges(
        xb.at[0], own,
        erecv[0].astype(F32).reshape(rows, 8, width), erecv[1].astype(F32).reshape(rows, 8, width),
    )
    for copy in row_copies(1) + row_copies(2):
        copy.start()

    def row_mask(first, count):
        on = mp[pl.ds(first, count)][:, :1, :]
        return jnp.concatenate([on, on], axis=2)

    def norm(cells, blk):
        mean_of = jnp.full((width, width), 1.0 / width, BF)
        off = cells.astype(F32) - jnp.dot(cells, mean_of, preferred_element_type=F32)
        var = jnp.dot((off * off).astype(BF), mean_of, preferred_element_type=F32)
        return (off * lax.rsqrt(var + 1e-05) * gain[pl.ds(blk, 1)]).astype(BF)

    column = lax.broadcasted_iota(jnp.int32, (1, wide, 1), 1)
    inside = (column >= EDGE) & (column < EDGE + cols)

    spare = BLOCKS + 1

    def state_copy(blk, i, to_blk, r, to):
        return remote(
            att.at[blk, i], xb.at[to_blk, EDGE + r], h_send.at[blk, i], x_recv.at[to_blk, r], to
        )

    def block(blk):
        x = xb.at[blk]
        w1_copy, w2_copy, wqkv_copy, wo_copy = weight_copies(blk)
        band = lat + blk * (band_1 - lat)
        sector = lon + blk * (sector_1 - lon)
        parity = sector % 2
        first_row = band % 2 * rows

        def arrived(r):
            @pl.when(elsewhere((band_1, r * CORES + sector_1 % 2)))
            def _():
                state_copy(0, 0, 1, r, (lat, sibling)).wait_recv()

        w1_copy.wait()

        @pl.when(blk == 1)
        def _():
            to_up, to_down = row_copies(3)
            each(EDGE, arrived)
            to_up.start()
            each(EDGE, lambda r: arrived(rows - EDGE + r))
            to_down.start()
            each(rows - 2 * EDGE, lambda r: arrived(EDGE + r))

        def first(start, count):
            got = conv(x, start, count, 1, w1.at[blk])
            got = jax.nn.gelu(got).reshape(count, wide, width) * row_mask(first_row + start + 1, count)
            hb[pl.ds(start, count)] = got.astype(BF)

        first(EDGE, rows - 2)

        def outer(side):
            def ready(n):
                @pl.when(side == 0)
                def _():
                    row_copies(n)[1].wait_recv()

                @pl.when(side == 1)
                def _():
                    row_copies(n)[0].wait_recv()

            @pl.when(blk == 0)
            def _():
                for n in range(3):
                    ready(n)

            @pl.when(blk == 1)
            def _():
                ready(3)

            @pl.when((side == 0) & (band == 0))
            def _():
                x[0:EDGE] = jnp.zeros((EDGE, wide, width), BF)

            @pl.when((side == 1) & (band == lats - 1))
            def _():
                x[EDGE + rows :] = jnp.zeros((EDGE, wide, width), BF)

            first(3 * EDGE * side, EDGE)

        w2_copy.wait()

        def row_copy(r):
            return remote(
                nself.at[blk, r], nbuf.at[blk, parity, sector // 2], f_send.at[blk, r],
                f_recv.at[blk, sector // 2], (band, r * CORES + parity),
            )

        @pl.when(blk == 0)
        def _():
            mask_copy().wait_recv()

        def second(k):
            side = (1 - core + k // 2) % 2
            a = side * 4 + (x_at + 1 + side + x_at // 2 + k) % 2 * 2

            @pl.when(k % 2 == 0)
            def _():
                outer(side)

            got = jax.nn.gelu(conv(hb, a, 2, 2, w2.at[blk])).reshape(2, wide, width)
            got = (x[pl.ds(a + EDGE, 2)].astype(F32) + got) * row_mask(first_row + a + EDGE, 2)
            nself[blk, pl.ds(a, 2)] = got.astype(BF)
            for i in range(2):
                r = a + i
                far = elsewhere((band, r * CORES + parity))

                @pl.when(far)
                def _():
                    row_copy(r).start()

                @pl.when(jnp.logical_not(far))
                def _():
                    nbuf[blk, parity, sector // 2] = nself[blk, r]

        each(groups, second)

        def half_copy(i):
            slot = nbuf.at[blk, core, i]
            return remote(slot, slot, s_send.at[blk, i], s_recv.at[blk, i], (lat, sibling))

        def pass_on(k):
            i = across(k // 2) * 2 + k % 2

            @pl.when(elsewhere(placed(blk, lat, i * CORES + core)))
            def _():
                remote(
                    nself.at[blk, i], nbuf.at[blk, core, i], f_send.at[blk, i], f_recv.at[blk, i],
                    (lat, sibling),
                ).wait_recv()

            half_copy(i).start()

        each(chips, pass_on)

        wqkv_copy.wait()
        first_head = lax.broadcasted_iota(jnp.int32, (1, 1, 2 * head_dim), 2) < head_dim
        ones = jnp.where(inside, 1.0, 0.0)

        scale = math.log2(math.e) / math.sqrt(head_dim)

        def query(cells):
            found = jnp.dot(cells, wqkv[blk, :, :width], preferred_element_type=F32)
            return (found * scale).astype(BF).reshape(chips, -1, width)

        def keys_values(t):
            side = (core + t) % CORES

            @pl.when(t == 1)
            def _():
                each(chips, lambda i: half_copy(i).wait_recv())

            cells = norm(nbuf[blk, side].reshape(half, width), blk)

            @pl.when(t == 0)
            def _():
                qb[...] = query(cells)

            cells = jnp.where(inside, cells.reshape(chips, wide, width), jnp.zeros((), BF))
            cells = cells.reshape(half, width)
            both = jnp.dot(cells, wqkv[blk, :, width:], preferred_element_type=F32)
            kb[side] = both[:, :width].astype(BF).reshape(chips, wide, width)
            values = both[:, width:].reshape(chips, wide, width)
            for h in range(HEADS):
                pair = values[:, :, h // 2 * 2 * head_dim :][:, :, : 2 * head_dim]
                keep = first_head if h % 2 == 0 else ~first_head
                vx[h, side] = jnp.where(keep, pair, ones).astype(BF).reshape(vx.shape[2:])

        qm[...] = nbuf[blk, core]
        each(CORES, keys_values)

        def join(i):
            before, after = (i + chips - 1 + core) % chips, (i + core) % chips
            from_left = shifted(nbuf[blk, 1 - core, pl.ds(before, 1)], wide - 8, 6)
            from_right = shifted(nbuf[blk, 1 - core, pl.ds(after, 1)], 0, 2)
            with_edges(qm, pl.ds(i, 1), from_left, from_right)

        @pl.when(blk < BLOCKS - 1)
        def _():
            for i in range(chips):
                join(i)
            for ends in (slice(0, 16), slice(wide - 16, wide)):
                qb[:, ends] = query(norm(qm[:, ends].reshape(chips * 16, width), blk))

        wo_copy.wait()

        def home_copy(i):
            to = placed(1 - blk, lat, i * CORES + core)
            stays = jnp.where(elsewhere(to), 0, 1)
            return remote(
                att.at[blk, i],
                xb.at[blk + 1 + stays * (spare - blk - 1), EDGE + chip + stays * (blk - EDGE - chip)],
                h_send.at[blk, i],
                x_recv.at[blk + 1 + stays * (spare - blk - 1), chip + stays * (blk - chip)],
                (to[0], to[1] + stays * (sibling - to[1])),
            )

        def keep(i):
            @pl.when(jnp.logical_not(elsewhere(placed(1 - blk, lat, i * CORES + core))))
            def _():
                xb[blk + 1, EDGE + chip] = att[blk, i]

        def attend(k):
            a = across(k) * 2
            query = qb[pl.ds(a, 2)].reshape(2 * wide, width)
            low_lane = lax.broadcasted_iota(jnp.int32, (1, 2 * head_dim), 1) < head_dim
            zero = jnp.zeros((), BF)
            attended = []
            for p in range(HEADS // 2):
                span = slice(p * 2 * head_dim, (p + 1) * 2 * head_dim)
                both = query[:, span]
                lhs = jnp.concatenate(
                    [jnp.where(low_lane, both, zero), jnp.where(low_lane, zero, both)], axis=0
                )
                keys = kb[:, :, :, span].reshape(CORES * half, 2 * head_dim)
                scores = lax.dot_general(
                    lhs, keys, (((1,), (1,)), ((), ())), preferred_element_type=F32
                )
                expo = jnp.exp2(scores).astype(BF)
                got = []
                for e in range(2):
                    values = vx[2 * p + e].reshape(CORES * half, 2 * head_dim)
                    part = jnp.dot(
                        expo[e * 2 * wide : (e + 1) * 2 * wide], values, preferred_element_type=F32
                    )
                    got.append(part / pltpu.roll(part, head_dim, 1))
                attended.append(jnp.where(low_lane, got[0], got[1]).astype(BF))
            update = jnp.dot(
                jnp.concatenate(attended, axis=1), wo[blk], preferred_element_type=F32
            )
            state = qm[pl.ds(a, 2)].astype(F32) + update.reshape(2, wide, width)
            state = state * row_mask(EDGE + y_hi * rows + chip, 1)
            att[blk, pl.ds(a, 2)] = state.astype(BF)
            home_copy(a).start()
            home_copy(a + 1).start()

        def attend_two(k):
            attend(2 * k)
            attend(2 * k + 1)

        each(groups // 2, attend_two)
        for n in range(2):
            keep(x_at * 2 + n)

    each(BLOCKS, block)

    def sent(blk):
        band = lat + blk * (band_1 - lat)
        parity = (lon + blk * (sector_1 - lon)) % 2

        def one(i):
            @pl.when(elsewhere((band, i * CORES + parity)))
            def _():
                remote(
                    nself.at[blk, i], nbuf.at[blk, core, i], f_send.at[blk, i], f_recv.at[blk, i], (lat, sibling)
                ).wait_send()

            slot = nbuf.at[blk, core, i]
            remote(slot, slot, s_send.at[blk, i], s_recv.at[blk, i], (lat, sibling)).wait_send()

            state_copy(blk, i, blk + 1, chip, (lat, sibling)).wait_send()

        each(chips, one)

    each(BLOCKS, sent)

    for copy in edge_copies() + sum((row_copies(n) for n in range(4)), []) + [mask_copy()]:
        copy.wait_send()

    def come_home(r):
        @pl.when(r != chip)
        def _():
            state_copy(0, 0, BLOCKS, r, (lat, sibling)).wait_recv()

    each(rows, come_home)

    def spared(blk):
        remote(
            att.at[0, 0], xb.at[spare, blk], h_send.at[0, 0], x_recv.at[spare, blk], (lat, sibling)
        ).wait_recv()

    for n in range(2):
        to = place_1(lat, (x_at * 2 + n) * CORES + 1 - core)

        @pl.when((to[0] == lat) & (to[1] == sibling))
        def _():
            spared(0)

    spared(1)
    out[...] = xb[BLOCKS, own]


def body(fields, lat_mask, conv_first, conv_second, norm_gain, qkv_weight, out_weight):
    rows, cols, width = fields.shape
    wide = cols + 2 * EDGE
    chips = lax.axis_size("lon") // CORES
    head_dim = width // HEADS
    vmem = pl.BlockSpec(memory_space=pltpu.VMEM)
    hbm = pl.BlockSpec(memory_space=pltpu.HBM)
    dma = pltpu.SemaphoreType.DMA
    wide_out = pl.pallas_call(
        kernel,
        out_shape=pltpu.VMEM((rows, wide, width), BF),
        in_specs=[hbm] * 7,
        out_specs=vmem,
        scratch_shapes=[
            pltpu.VMEM((cols, rows, width), BF),
            pltpu.SMEM(lat_mask.shape, jnp.int32),
            pltpu.VMEM(norm_gain.shape, F32),
            pltpu.VMEM(conv_first.shape, BF),
            pltpu.VMEM(conv_second.shape, BF),
            pltpu.VMEM(qkv_weight.shape, BF),
            pltpu.VMEM(out_weight.shape, BF),
            pltpu.VMEM((wide, rows, width), F32),
            pltpu.VMEM((BLOCKS + 2, rows + 2 * EDGE, wide, width), BF),
            pltpu.VMEM((rows + 4, wide, width), BF),
            pltpu.VMEM((2 * rows + 2 * EDGE, 8, width // 2), F32),
            pltpu.VMEM((2, rows * 8, width), BF),
            pltpu.VMEM((2, rows * 8, width), BF),
            pltpu.VMEM((BLOCKS, rows, wide, width), BF),
            pltpu.VMEM((BLOCKS, CORES, chips, wide, width), BF),
            pltpu.VMEM((chips, wide, width), BF),
            pltpu.VMEM((chips, wide, width), BF),
            pltpu.VMEM((CORES, chips, wide, width), BF),
            pltpu.VMEM((HEADS, CORES, chips, wide, 2 * head_dim), BF),
            pltpu.VMEM((BLOCKS, chips, wide, width), BF),
            dma((3,)),
            dma((4, BLOCKS)),
            dma((2,)),
            dma((2,)),
            dma((4, 2)),
            dma((4, 2)),
            dma((2,)),
            dma((BLOCKS, rows)),
            dma((BLOCKS, chips)),
            dma((BLOCKS, chips)),
            dma((BLOCKS, chips)),
            dma((BLOCKS, chips)),
            dma((BLOCKS + 2, rows)),
        ],
        compiler_params=pltpu.CompilerParams(
            collective_id=0, has_side_effects=True, vmem_limit_bytes=60 * 1024 * 1024
        ),
    )(jnp.transpose(fields, (1, 0, 2)), lat_mask, conv_first, conv_second, norm_gain, qkv_weight, out_weight)
    return wide_out[:, EDGE : EDGE + cols]


def solution(mesh):
    placed = (P("lat", "lon", None), P("lat"), P(), P(), P(), P(), P())
    return jax.shard_map(
        body, mesh=mesh, in_specs=placed, out_specs=P("lat", "lon", None), check_vma=False
    )
```
